128 devices in a mesh: dp: 16 (over x, y_lo, core), tensor: 8 (over y_hi, z).
Axes of the slice: x: 4, y: 4 (y_hi: 2, y_lo: 2; y = y_hi * 2 + y_lo), z: 4, core: 2. Of those that a mesh axis runs over, the one named last changes fastest.
Arguments:
- tokens: bfloat16 [32768, 4096], P(('dp', 'tensor')), may hold values from -100 to 100
- out_grads: bfloat16 [32768, 16384], P('dp', 'tensor'), may hold values from -100 to 100
- gradient: float32 [4096, 16384], P('dp', 'tensor'), may hold values from -6 to 6
- owners: int32 [8, 24], P('tensor'), may hold values from 0 to 15, as said below
Outputs:
- preconditioned: float32 [4096, 16384], P('dp', 'tensor')
- inverses: float32 [8, 16, 3, 256, 256], P('tensor', 'dp')
The draws below stay inside these ranges and needn't reach their ends.
Inputs may be any that keep to these rules, and one draw needn't show every extreme that they name: `owners`: for each tensor index no owner is named by more than 3 of the 24 blocks, and one owner is named by exactly 3.
All inputs are finite; a program needn't handle non-finite values. Where the reference program divides by a largest or mean magnitude, that divisor is 1e-20 or more.
Results may differ from the reference program's by a relative error of at most 0.0003.
Values may be sent and summed in bfloat16 or wider, within the bound.
A program may use at most 128 MiB of HBM per device.

```python
import math
import jax
import jax.numpy as jnp
from jax import lax

D = 4096
FF = 16384
BLOCK = 256
NS_ITERS = 12
TOKENS = 32768
A_BLOCKS = 16
G_BLOCKS = 64
GROUP_BLOCKS = 8
FACTORS = 24
MAXOWN = 3
N_DP = 16
N_TENSOR = 8


def banded_field(noise_field, column_key, row_scale):
    column_scale = jnp.exp(jax.random.uniform(column_key, (1, noise_field.shape[1]), jnp.float32, math.log(0.5), math.log(5.0)))
    mixed = noise_field + 0.8 * jnp.roll(noise_field, -1, axis=1) + 0.5 * jnp.roll(noise_field, -3, axis=1)
    return mixed * column_scale * row_scale


def draw_field(key, row_count, column_count, row_spread):
    noise_key, column_key, row_key = jax.random.split(key, 3)
    noise_field = jnp.clip(jax.random.normal(noise_key, (row_count, column_count), jnp.float32), -4.0, 4.0)
    row_scale = jnp.exp(jax.random.uniform(row_key, (row_count, 1), jnp.float32, -row_spread, row_spread))
    return banded_field(noise_field, column_key, row_scale)


def draw_tokens(key, part):
    key = jax.random.fold_in(key, 11)
    field = draw_field(key, TOKENS, D, 0.0)
    return field.astype(jnp.bfloat16)


def draw_out_grads(key, part):
    key = jax.random.fold_in(key, 23)
    field = draw_field(key, TOKENS, FF, 0.0)
    return field.astype(jnp.bfloat16)


def assign_group(group_key):
    busiest_key, order_key, rest_key = jax.random.split(group_key, 3)
    busiest = jax.random.randint(busiest_key, (), 0, N_DP)
    block_order = jax.random.permutation(order_key, FACTORS)
    remaining = (busiest + 1 + jax.random.permutation(rest_key, N_DP - 1)) % N_DP
    position = jnp.arange(FACTORS, dtype=jnp.int32)
    chosen = jnp.where(position < MAXOWN, busiest, remaining[jnp.maximum(position - MAXOWN, 0) % (N_DP - 1)])
    return jnp.zeros((FACTORS,), jnp.int32).at[block_order].set(chosen.astype(jnp.int32))


def draw_owners(key, part):
    key = jax.random.fold_in(key, 37)
    group_keys = jax.random.split(key, N_TENSOR)
    return jax.vmap(assign_group)(group_keys)


def levels(stream_key, dims, cuts, smallest, largest):
    loudness, own = 1.0, jax.random.fold_in(stream_key, 6)
    for dim, parts in cuts:
        steps = jnp.exp(jax.random.uniform(jax.random.fold_in(own, dim), (parts,), jnp.float32, smallest / len(cuts), largest / len(cuts)))
        loudness = loudness * jnp.repeat(steps, dims[dim] // parts).reshape([-1 if axis == dim else 1 for axis in range(len(dims))])
    return loudness


def normal_values(stream_key, dims, deviation, bound, shards=(), held_as=jnp.bfloat16):
    array = deviation * jax.random.normal(stream_key, dims, jnp.float32)
    if shards:
        array = array * levels(stream_key, dims, shards, -0.22, 0.18)
    return jnp.clip(array, -bound, bound).astype(held_as)


def setup_inputs(seed: int = 0) -> dict:
    splits = jax.random.split(jax.random.key(seed), 5)
    tokens = draw_tokens(jax.random.fold_in(splits[4], 71), 0)
    out_grads = draw_out_grads(jax.random.fold_in(splits[4], 71), 0)
    gradient = normal_values(splits[2], (D, FF), 1.0, 6.0, ((0, 16), (1, 8)), jnp.float32)
    owners = draw_owners(jax.random.fold_in(splits[4], 71), 0)
    return dict(tokens=tokens, out_grads=out_grads, gradient=gradient, owners=owners)


damping_ratio = 0.01


def newton_inverse(covariance, live_slots):
    block_order = covariance.shape[-1]
    identity_matrix = jnp.eye(block_order, dtype=jnp.float32)
    diag_trace = jnp.sum(covariance * identity_matrix, axis=(1, 2))
    damped = covariance + (damping_ratio / block_order) * diag_trace[:, None, None] * identity_matrix
    damped = jnp.where(live_slots[:, None, None], damped, identity_matrix)
    row_bound = jnp.max(jnp.sum(jnp.abs(damped), axis=2), axis=1)
    initial = identity_matrix[None, :, :] / row_bound[:, None, None]

    def sweep(sweep_index, iterate):
        product = jnp.einsum('sij,sjk->sik', damped, iterate, precision=lax.Precision.HIGHEST)
        return jnp.einsum('sij,sjk->sik', iterate, 2.0 * identity_matrix - product, precision=lax.Precision.HIGHEST)

    result = lax.fori_loop(0, NS_ITERS, sweep, initial)
    return jnp.where(live_slots[:, None, None], result, jnp.float32(0.0))


def owner_selection(owner_row, owner_count, slot_count):
    listed = owner_row.shape[0]
    same_owner = owner_row[:, None] == owner_row[None, :]
    positions = jnp.arange(listed, dtype=jnp.int32)
    earlier = positions[None, :] < positions[:, None]
    slot_index = jnp.sum((same_owner & earlier).astype(jnp.int32), axis=1).astype(jnp.int32)
    target = owner_row.astype(jnp.int32) * slot_count + slot_index
    slots = jnp.arange(owner_count * slot_count, dtype=jnp.int32)
    return (slots[:, None] == target[None, :]).astype(jnp.float32)


def block_covariance(data, count):
    def one_block(block_index):
        column_block = lax.dynamic_slice_in_dim(data, block_index * BLOCK, BLOCK, 1)
        return jnp.dot(column_block.T, column_block, preferred_element_type=jnp.float32)

    return lax.map(one_block, jnp.arange(count, dtype=jnp.int32))


def reference(tokens, out_grads, gradient, owners):
    a_cov = block_covariance(tokens, A_BLOCKS) / jnp.float32(TOKENS)
    g_cov = block_covariance(out_grads, G_BLOCKS) / jnp.float32(TOKENS)
    a_inv = newton_inverse(a_cov, jnp.ones((A_BLOCKS,), dtype=bool))
    g_inv = newton_inverse(g_cov, jnp.ones((G_BLOCKS,), dtype=bool))
    grad_blocks = gradient.reshape(A_BLOCKS, BLOCK, G_BLOCKS, BLOCK)
    left_applied = jnp.einsum('aij,ajgk->aigk', a_inv, grad_blocks, precision=lax.Precision.HIGHEST)
    right_applied = jnp.einsum('aigk,gkl->aigl', left_applied, g_inv, precision=lax.Precision.HIGHEST)
    preconditioned = right_applied.reshape(D, FF)

    def group_inverses(inputs):
        group_index, owner_row = inputs
        g_part = lax.dynamic_slice_in_dim(g_inv, group_index * GROUP_BLOCKS, GROUP_BLOCKS, 0)
        factor_list = jnp.concatenate([a_inv, g_part], axis=0)
        selector = owner_selection(owner_row, N_DP, MAXOWN)
        placed = jnp.einsum('ob,bij->oij', selector, factor_list, precision=lax.Precision.HIGHEST)
        return placed.reshape(N_DP, MAXOWN, BLOCK, BLOCK)

    inverses = lax.map(group_inverses, (jnp.arange(N_TENSOR, dtype=jnp.int32), owners))
    return preconditioned, inverses
```

```python
import functools
import jax
import jax.numpy as jnp
from jax import lax
from jax.experimental import pallas as pl
from jax.experimental.pallas import tpu as pltpu
from jax.sharding import PartitionSpec as P

BLOCK = 256
HALF = 128
ROWS = 264
CUT = 136
NS_ITERS = 12
DAMPING = 0.01
MESH = pl.DeviceIdType.MESH
F32 = jnp.float32
BF16 = jnp.bfloat16


def iotas(n):
    return (
        lax.broadcasted_iota(jnp.int32, (n, n), 0),
        lax.broadcasted_iota(jnp.int32, (n, n), 1),
    )


def pack_into(dst, full):
    row, col = iotas(HALF)
    upper_left, lower_right = full[:HALF, :HALF], full[HALF:, HALF:]
    dst[0:HALF, :] = jnp.where(row >= col, upper_left, lower_right)
    dst[HALF:BLOCK, :] = full[HALF:, :HALF]
    diagonal = jnp.sum(jnp.where(row == col, lower_right, 0.0), axis=0, keepdims=True)
    dst[BLOCK:ROWS, :] = jnp.broadcast_to(diagonal, (ROWS - BLOCK, HALF))


def unpack_into(dst, packed):
    row, col = iotas(HALF)
    both, below = packed[0:HALF, :], packed[HALF:BLOCK, :]
    diagonal = packed[BLOCK:BLOCK + 1, :]
    turned = both.T
    dst[0:HALF, 0:HALF] = jnp.where(row >= col, both, turned)
    dst[HALF:BLOCK, HALF:BLOCK] = jnp.where(row < col, both, jnp.where(row == col, diagonal, turned))
    dst[HALF:BLOCK, 0:HALF] = below
    dst[0:HALF, HALF:BLOCK] = below.T


def bdot(a, b):
    return jnp.dot(a, b, preferred_element_type=F32)


def gram(v):
    return lax.dot_general(v, v, (((0,), (0,)), ((), ())), preferred_element_type=F32)


def split2(v):
    high = v.astype(BF16)
    return high, (v - high.astype(F32)).astype(BF16)


def split3(v):
    high = v.astype(BF16)
    rest = v - high.astype(F32)
    mid = rest.astype(BF16)
    return high, mid, (rest - mid.astype(F32)).astype(BF16)


def dot3(a, b):
    ah, al = split2(a)
    bh, bl = split2(b)
    return (bdot(ah, bl) + bdot(al, bh)) + bdot(ah, bh)


def newton_inverse(full, state, total_tokens):
    row, col = iotas(BLOCK)
    on_diagonal = row == col
    cov = full[...] * (1.0 / total_tokens)
    trace = jnp.sum(jnp.where(on_diagonal, cov, 0.0))
    damped = cov + jnp.where(on_diagonal, DAMPING / BLOCK * trace, 0.0)
    bound = jnp.max(jnp.sum(jnp.abs(damped), axis=0, keepdims=True), axis=1, keepdims=True)
    p = damped / bound
    state[BLOCK:, :] = jnp.where(on_diagonal, 2.0, 0.0) - p
    state[:BLOCK, :] = 2.0 * p - jnp.dot(p, p, precision=lax.Precision.HIGHEST)

    def sweep(index, carry):
        p, x = state[:BLOCK, :], state[BLOCK:, :]
        ph, pm, pl_ = split3(p)
        xh, xm = split2(x)
        by_high = bdot(jnp.concatenate([pl_, pm, ph, xm, xh], 0), ph)
        by_mid = bdot(jnp.concatenate([pm, ph, xh], 0), pm)
        by_low = bdot(ph, pl_)
        n = BLOCK
        pp = ((by_low + by_high[:n] + by_mid[:n]) + (by_high[n:2 * n] + by_mid[n:2 * n])) + by_high[2 * n:3 * n]
        xp = (by_high[3 * n:4 * n] + by_mid[2 * n:]) + by_high[4 * n:]
        state[:BLOCK, :] = 2.0 * p - pp
        state[BLOCK:, :] = 2.0 * x - xp
        return carry

    lax.fori_loop(0, NS_ITERS - 2, sweep, 0)
    p, x = state[:BLOCK, :], state[BLOCK:, :]
    return (2.0 * x - dot3(x, p)) / bound


def factor_kernel(
    total_tokens,
    tokens,
    out_grads,
    a_all,
    g_all,
    tok,
    grads,
    a_part,
    g_part,
    a_relay,
    a_ring,
    a_sum,
    a_second,
    a_line,
    a_third,
    g_core,
    g_relay,
    g_ring,
    g_sum,
    g_other,
    ns_in,
    full,
    state,
    load_sem,
    send_sem,
    recv_sem,
):
    dp, tensor = lax.axis_index("dp"), lax.axis_index("tensor")
    x, y_lo, c = dp // 4, (dp // 2) % 2, dp % 2
    y_hi, z = tensor // 4, tensor % 4
    y = y_hi * 2 + y_lo
    o = 1 - c

    def device(x_, y_, z_, c_):
        return {"dp": x_ * 4 + (y_ % 2) * 2 + c_, "tensor": (y_ // 2) * 4 + z_}

    first, second = o * z + c * y, o * y + c * z

    def plane(first_, second_):
        return device(x, c * first_ + o * second_, o * first_ + c * second_, c)

    def along_x(x_):
        return device(x_, y, z, c)

    other_core = device(x, y, z, o)
    y_partner = device(x, y_hi * 2 + 1 - y_lo, z, c)

    def step(position, by):
        return (position + 4 + by) % 4

    sent = []
    counters = {"send": 0, "recv": 0}

    def take(kind, count=1):
        at = counters[kind]
        counters[kind] += count
        return at

    def send(src, dst, recv_at, target, cond=None):
        send_at = take("send")

        def make():
            return pltpu.make_async_remote_copy(
                src_ref=src, dst_ref=dst, send_sem=send_sem.at[send_at], recv_sem=recv_sem.at[recv_at],
                device_id=target, device_id_type=MESH,
            )

        if cond is None:
            make().start()
        else:
            pl.when(cond)(lambda: make().start())
        sent.append((make, cond))

    def await_recv(dst, recv_at):
        pltpu.make_async_remote_copy(
            src_ref=dst, dst_ref=dst, send_sem=send_sem.at[0], recv_sem=recv_sem.at[recv_at],
            device_id=other_core, device_id_type=MESH,
        ).wait_recv()

    def mine(q):
        return 2 * q + (c + q) % 2

    def theirs(q):
        return 2 * q + (o + q) % 2

    own_tokens = pltpu.make_async_copy(
        tokens.at[:, pl.ds(pl.multiple_of(c * 2048, 2048), 2048)], tok.at[0], load_sem.at[8]
    )
    own_tokens.start()

    def grad_load(block, at):
        return pltpu.make_async_copy(
            out_grads.at[:, pl.ds(pl.multiple_of(block * BLOCK, BLOCK), BLOCK)], grads.at[at], load_sem.at[at]
        )

    order = [theirs(q) for q in range(4)] + [mine(step(x, by)) for by in (2, 1, 3, 0)]
    for at, block in enumerate(order):
        grad_load(block, at).start()

    barrier = pltpu.get_barrier_semaphore()
    others = [other_core]
    for by in (1, 2, 3):
        others += [
            device(step(x, by), y, z, c),
            device(x, step(y, by), z, c),
            device(x, y, step(z, by), c),
        ]
    for target in others:
        pl.semaphore_signal(barrier, inc=1, device_id=target, device_id_type=MESH)
    pl.semaphore_wait(barrier, len(others))

    token_recv = take("recv")
    send(tokens.at[:, pl.ds(pl.multiple_of(o * 2048, 2048), 2048)], tok.at[1], token_recv, other_core)

    core_recv = take("recv", 4)
    for q in range(4):
        grad_load(order[q], q).wait()
        pack_into(g_part.at[q], gram(grads[q]))
        send(g_part.at[q], g_core.at[q], core_recv + q, other_core)

    own_tokens.wait()
    await_recv(tok.at[1], token_recv)

    def a_block(f, u):
        return f * 2 + u

    def a_gram(f, u):
        at = a_block(f, u)
        columns = pl.ds(pl.multiple_of(at * BLOCK, BLOCK), BLOCK)
        pack_into(a_part.at[at], gram(tok[0, :, columns]) + gram(tok[1, :, columns]))
        return a_part.at[at]

    up, down, far = step(first, 1), step(first, -1), step(first, 2)
    relay_recv = take("recv", 2)
    ring_recv = take("recv", 4)
    send(a_gram(far, 0), a_relay.at[0], relay_recv, plane(up, second))
    send(a_gram(far, 1), a_relay.at[1], relay_recv + 1, plane(down, second))
    send(a_gram(up, 1), a_ring.at[1], ring_recv + 1, plane(up, second))
    send(a_gram(down, 0), a_ring.at[2], ring_recv + 2, plane(down, second))
    a_gram(up, 0)
    a_gram(down, 1)
    a_gram(first, 0)
    a_gram(first, 1)

    x_up, x_down, x_far = step(x, 1), step(x, -1), step(x, 2)
    g_relay_recv = take("recv", 2)
    g_ring_recv = take("recv", 4)
    top, bottom = pl.ds(0, CUT), pl.ds(CUT, ROWS - CUT)

    def g_gram(at, q):
        grad_load(order[at], at).wait()
        pack_into(g_part.at[at], gram(grads[at]))
        return q

    for at, q in ((4, x_far), (5, x_up), (6, x_down), (7, x)):
        g_gram(at, q)
        if at == 4:
            for k in range(4):
                await_recv(g_core.at[k], core_recv + k)
        g_part[at] += g_core[q]
        if at == 4:
            send(g_part.at[4, top], g_relay.at[top], g_relay_recv, along_x(x_up))
            send(g_part.at[4, bottom], g_relay.at[bottom], g_relay_recv + 1, along_x(x_down))
        if at == 5:
            send(g_part.at[5, bottom], g_ring.at[0, bottom], g_ring_recv, along_x(x_up))
        if at == 6:
            send(g_part.at[6, top], g_ring.at[1, top], g_ring_recv + 1, along_x(x_down))

    await_recv(a_relay.at[0], relay_recv)
    a_part[a_block(up, 0)] += a_relay[0]
    send(a_part.at[a_block(up, 0)], a_ring.at[0], ring_recv, plane(up, second))
    await_recv(a_relay.at[1], relay_recv + 1)
    a_part[a_block(down, 1)] += a_relay[1]
    send(a_part.at[a_block(down, 1)], a_ring.at[3], ring_recv + 3, plane(down, second))

    await_recv(g_relay.at[top], g_relay_recv)
    g_part[5, top] += g_relay[top]
    send(g_part.at[5, top], g_ring.at[0, top], g_ring_recv + 2, along_x(x_up))
    await_recv(g_relay.at[bottom], g_relay_recv + 1)
    g_part[6, bottom] += g_relay[bottom]
    send(g_part.at[6, bottom], g_ring.at[1, bottom], g_ring_recv + 3, along_x(x_down))

    second_recv = take("recv", 3)
    for u in range(2):
        await_recv(a_ring.at[u], ring_recv + u)
        await_recv(a_ring.at[2 + u], ring_recv + 2 + u)
        a_sum[u] = a_part[a_block(first, u)] + a_ring[u] + a_ring[2 + u]
        slot = step(second, -2 * u) - 1
        send(a_sum.at[u], a_second.at[slot], second_recv + slot, plane(first, jnp.int32(2 * u)), second != 2 * u)

    g_ring_recvs = ((0, bottom, 0), (1, top, 1), (0, top, 2), (1, bottom, 3))
    for slot, part, k in g_ring_recvs:
        await_recv(g_ring.at[slot, part], g_ring_recv + k)
    g_sum[...] = g_part[7] + g_ring[0] + g_ring[1]
    g_owner = y_lo == (c + x) % 2
    y_recv = take("recv")
    send(g_sum, g_other, y_recv, y_partner, jnp.logical_not(g_owner))

    on_line = second % 2 == 0
    u_line = second // 2
    x_owner = o * (2 * u_line + 1) + c * first
    a_owner = jnp.logical_and(on_line, x == x_owner)
    third_recv = take("recv", 3)

    @pl.when(on_line)
    def _():
        for k in range(3):
            await_recv(a_second.at[k], second_recv + k)
        a_line[...] = a_sum[u_line] + a_second[0] + a_second[1] + a_second[2]

    third_slot = step(x, -x_owner) - 1
    send(
        a_line, a_third.at[third_slot], third_recv + third_slot, along_x(x_owner),
        jnp.logical_and(on_line, x != x_owner),
    )

    @pl.when(g_owner)
    def _():
        await_recv(g_other, y_recv)
        ns_in[...] = g_sum[...] + g_other[...]

    @pl.when(a_owner)
    def _():
        for k in range(3):
            await_recv(a_third.at[k], third_recv + k)
        ns_in[...] = a_line[...] + a_third[0] + a_third[1] + a_third[2]

    g_mine = mine(x)
    a_mine = c * 8 + a_block(first, u_line)

    @pl.when(jnp.logical_or(g_owner, a_owner))
    def _():
        unpack_into(full, ns_in[...])
        full[...] = newton_inverse(full, state, total_tokens)

        @pl.when(g_owner)
        def _():
            pack_into(g_all.at[g_mine], full[...])

        @pl.when(a_owner)
        def _():
            pack_into(a_all.at[a_mine], full[...])

    inv_y_recv = take("recv")
    send(g_all.at[g_mine], g_all.at[g_mine], inv_y_recv, y_partner, g_owner)
    a_x_recv = take("recv")
    for by in (1, 3, 2):
        target = step(x, by)
        send(a_all.at[a_mine], a_all.at[a_mine], a_x_recv, along_x(target), a_owner)

    @pl.when(jnp.logical_not(g_owner))
    def _():
        await_recv(g_all.at[g_mine], inv_y_recv)

    g_x_recv = take("recv", 4)
    g_core_recv = take("recv", 4)
    send(g_all.at[g_mine], g_all.at[g_mine], g_x_recv, along_x(x_up))
    send(g_all.at[g_mine], g_all.at[g_mine], g_x_recv + 1, along_x(x_down))
    send(g_all.at[g_mine], g_all.at[g_mine], g_core_recv, other_core)
    from_down, from_up, from_far = g_all.at[mine(x_down)], g_all.at[mine(x_up)], g_all.at[mine(x_far)]
    await_recv(from_down, g_x_recv)
    send(from_down.at[top], from_down.at[top], g_x_recv + 2, along_x(x_up))
    send(from_down, from_down, g_core_recv + 1, other_core)
    await_recv(from_up, g_x_recv + 1)
    send(from_up.at[bottom], from_up.at[bottom], g_x_recv + 3, along_x(x_down))
    send(from_up, from_up, g_core_recv + 2, other_core)
    await_recv(from_far.at[top], g_x_recv + 2)
    await_recv(from_far.at[bottom], g_x_recv + 3)
    send(from_far, from_far, g_core_recv + 3, other_core)

    @pl.when(jnp.logical_and(on_line, x != x_owner))
    def _():
        await_recv(a_all.at[a_mine], a_x_recv)

    a_second_recv = take("recv", 2)
    for by in (1, 3, 2):
        send(
            a_all.at[a_mine], a_all.at[a_mine], a_second_recv + u_line, plane(first, step(second, by)), on_line
        )
    a_first_recv = take("recv", 6)
    a_core_recv = take("recv", 8)

    def held(f, u):
        return a_all.at[c * 8 + a_block(f, u)]

    for u in range(2):
        own = held(first, u)

        @pl.when(second != 2 * u)
        def _():
            await_recv(own, a_second_recv + u)

        send(own, own, a_first_recv + u, plane(up, second))
        send(own, own, a_first_recv + 2 + u, plane(down, second))
        send(own, own, a_core_recv + u, other_core)
    for u in range(2):
        from_below, from_above = held(down, u), held(up, u)
        await_recv(from_below, a_first_recv + u)
        if u == 0:
            send(from_below, from_below, a_first_recv + 4, plane(up, second))
        send(from_below, from_below, a_core_recv + 2 + u, other_core)
        await_recv(from_above, a_first_recv + 2 + u)
        if u == 1:
            send(from_above, from_above, a_first_recv + 5, plane(down, second))
        send(from_above, from_above, a_core_recv + 4 + u, other_core)
    for u in range(2):
        opposite = held(far, u)
        await_recv(opposite, a_first_recv + 4 + u)
        send(opposite, opposite, a_core_recv + 6 + u, other_core)

    for k, q in enumerate((x, x_down, x_up, x_far)):
        await_recv(g_all.at[theirs(q)], g_core_recv + k)
    for k, f in enumerate((second, step(second, -1), step(second, 1), step(second, 2))):
        for u in range(2):
            await_recv(a_all.at[o * 8 + a_block(f, u)], a_core_recv + 2 * k + u)

    for make, cond in sent:
        if cond is None:
            make().wait_send()
        else:
            pl.when(cond)(lambda make=make: make().wait_send())
    assert counters["send"] <= 64 and counters["recv"] <= 64, counters


def factors(tokens, out_grads, total_tokens):
    vmem = pl.BlockSpec(memory_space=pltpu.VMEM)
    anywhere = pl.BlockSpec(memory_space=pl.ANY)

    def packed(*lead):
        return pltpu.VMEM((*lead, ROWS, HALF), F32)

    return pl.pallas_call(
        functools.partial(factor_kernel, total_tokens),
        out_shape=(
            jax.ShapeDtypeStruct((16, ROWS, HALF), F32),
            jax.ShapeDtypeStruct((8, ROWS, HALF), F32),
        ),
        in_specs=[anywhere, anywhere],
        out_specs=(vmem, vmem),
        scratch_shapes=[
            pltpu.VMEM((2, 256, 2048), BF16),
            pltpu.VMEM((8, 2048, BLOCK), BF16),
            packed(8),
            packed(8),
            packed(2),
            packed(4),
            packed(2),
            packed(3),
            packed(),
            packed(3),
            packed(4),
            packed(),
            packed(2),
            packed(),
            packed(),
            packed(),
            pltpu.VMEM((BLOCK, BLOCK), F32),
            pltpu.VMEM((2 * BLOCK, BLOCK), F32),
            pltpu.SemaphoreType.DMA((9,)),
            pltpu.SemaphoreType.DMA((64,)),
            pltpu.SemaphoreType.DMA((64,)),
        ],
        compiler_params=pltpu.CompilerParams(
            collective_id=0, has_side_effects=True, vmem_limit_bytes=48 * 2**20
        ),
        name="factors",
    )(tokens, out_grads)


def apply_kernel(owners, a_all, g_all, gradient, out, inverses, full, left):
    dp = lax.axis_index("dp")
    j = pl.program_id(0)

    @pl.when(j == 0)
    def _():
        unpack_into(left, a_all[dp])

    @pl.when(j < 3)
    def _():
        def scan(b, carry):
            seen, chosen = carry
            hit = owners[0, b] == dp
            chosen = jnp.where(jnp.logical_and(hit, seen == j), b, chosen)
            return seen + hit.astype(jnp.int32), chosen

        _, chosen = lax.fori_loop(0, 24, scan, (jnp.int32(0), jnp.int32(-1)))

        @pl.when(chosen < 0)
        def _():
            inverses[0, 0, j] = jnp.zeros((BLOCK, BLOCK), F32)

        @pl.when(jnp.logical_and(chosen >= 0, chosen < 16))
        def _():
            unpack_into(inverses.at[0, 0, j], a_all[chosen])

        @pl.when(chosen >= 16)
        def _():
            unpack_into(inverses.at[0, 0, j], g_all[chosen - 16])

    unpack_into(full, g_all[j])
    out[...] = dot3(dot3(left[...], gradient[...]), full[...])


def apply(owners, a_all, g_all, gradient):
    count = gradient.shape[1] // BLOCK
    whole = lambda *shape: pl.BlockSpec(shape, lambda j: (0,) * len(shape))
    return pl.pallas_call(
        apply_kernel,
        grid=(count,),
        out_shape=(
            jax.ShapeDtypeStruct(gradient.shape, F32),
            jax.ShapeDtypeStruct((1, 1, 3, BLOCK, BLOCK), F32),
        ),
        in_specs=[
            pl.BlockSpec(memory_space=pltpu.SMEM),
            whole(16, ROWS, HALF),
            whole(8, ROWS, HALF),
            pl.BlockSpec((BLOCK, BLOCK), lambda j: (0, j)),
        ],
        out_specs=(
            pl.BlockSpec((BLOCK, BLOCK), lambda j: (0, j)),
            whole(1, 1, 3, BLOCK, BLOCK),
        ),
        scratch_shapes=[pltpu.VMEM((BLOCK, BLOCK), F32), pltpu.VMEM((BLOCK, BLOCK), F32)],
        compiler_params=pltpu.CompilerParams(vmem_limit_bytes=32 * 2**20),
        name="apply",
    )(owners, a_all, g_all, gradient)


def on_device(tokens, out_grads, gradient, owners):
    total_tokens = tokens.shape[0] * lax.axis_size("tensor") * lax.axis_size("dp")
    a_all, g_all = factors(tokens, out_grads, total_tokens)
    return apply(owners, a_all, g_all, gradient)


def solution(mesh):
    placed = (P(("dp", "tensor"), None), P("dp", "tensor"), P("dp", "tensor"), P("tensor", None))
    return jax.shard_map(
        on_device,
        mesh=mesh,
        in_specs=placed,
        out_specs=(P("dp", "tensor"), P("tensor", "dp", None, None, None)),
        check_vma=False,
    )
```

```python
import functools
import jax
import jax.numpy as jnp
from jax import lax
from jax.experimental import pallas as pl
from jax.experimental.pallas import tpu as pltpu
from jax.sharding import PartitionSpec as P

BLOCK = 256
HALF = 128
PIECE = 136
ROWS = 2 * PIECE
NS_ITERS = 12
DAMPING = 0.01
MESH = pl.DeviceIdType.MESH
F32 = jnp.float32
BF16 = jnp.bfloat16


def iotas(n):
    return (
        lax.broadcasted_iota(jnp.int32, (n, n), 0),
        lax.broadcasted_iota(jnp.int32, (n, n), 1),
    )


def pack_into(top, bottom, full):
    row, col = iotas(HALF)
    upper_left, lower_right = full[:HALF, :HALF], full[HALF:, HALF:]
    top[0:HALF, :] = jnp.where(row >= col, upper_left, lower_right)
    diagonal = jnp.sum(jnp.where(row == col, lower_right, 0.0), axis=0, keepdims=True)
    top[HALF:PIECE, :] = jnp.broadcast_to(diagonal, (PIECE - HALF, HALF))
    bottom[0:HALF, :] = full[HALF:, :HALF]
    bottom[HALF:PIECE, :] = jnp.zeros((PIECE - HALF, HALF), F32)


def unpack_into(dst, packed):
    row, col = iotas(HALF)
    both, below = packed[0:HALF, :], packed[PIECE:PIECE + HALF, :]
    diagonal = packed[HALF:HALF + 1, :]
    turned = both.T
    dst[0:HALF, 0:HALF] = jnp.where(row >= col, both, turned)
    dst[HALF:BLOCK, HALF:BLOCK] = jnp.where(row < col, both, jnp.where(row == col, diagonal, turned))
    dst[HALF:BLOCK, 0:HALF] = below
    dst[0:HALF, HALF:BLOCK] = below.T


def bdot(a, b):
    return jnp.dot(a, b, preferred_element_type=F32)


def gram(v):
    return lax.dot_general(v, v, (((0,), (0,)), ((), ())), preferred_element_type=F32)


def split2(v):
    high = v.astype(BF16)
    return high, (v - high.astype(F32)).astype(BF16)


def split3(v):
    high = v.astype(BF16)
    rest = v - high.astype(F32)
    mid = rest.astype(BF16)
    return high, mid, (rest - mid.astype(F32)).astype(BF16)


def dot3(a, b):
    ah, al = split2(a)
    bh, bl = split2(b)
    return (bdot(ah, bl) + bdot(al, bh)) + bdot(ah, bh)


def newton_inverse(full, state, total_tokens):
    row, col = iotas(BLOCK)
    on_diagonal = row == col
    cov = full[...] * (1.0 / total_tokens)
    trace = jnp.sum(jnp.where(on_diagonal, cov, 0.0))
    damped = cov + jnp.where(on_diagonal, DAMPING / BLOCK * trace, 0.0)
    bound = jnp.max(jnp.sum(jnp.abs(damped), axis=0, keepdims=True), axis=1, keepdims=True)
    p = damped / bound
    state[BLOCK:, :] = jnp.where(on_diagonal, 2.0, 0.0) - p
    state[:BLOCK, :] = 2.0 * p - jnp.dot(p, p, precision=lax.Precision.HIGHEST)

    def sweep(index, carry):
        p, x = state[:BLOCK, :], state[BLOCK:, :]
        ph, pm, pl_ = split3(p)
        xh, xm = split2(x)
        by_high = bdot(jnp.concatenate([pl_, pm, ph, xm, xh], 0), ph)
        by_mid = bdot(jnp.concatenate([pm, ph, xh], 0), pm)
        by_low = bdot(ph, pl_)
        n = BLOCK
        pp = ((by_low + by_high[:n] + by_mid[:n]) + (by_high[n:2 * n] + by_mid[n:2 * n])) + by_high[2 * n:3 * n]
        xp = (by_high[3 * n:4 * n] + by_mid[2 * n:]) + by_high[4 * n:]
        state[:BLOCK, :] = 2.0 * p - pp
        state[BLOCK:, :] = 2.0 * x - xp
        return carry

    lax.fori_loop(0, NS_ITERS - 2, sweep, 0)
    p, x = state[:BLOCK, :], state[BLOCK:, :]
    return (2.0 * x - dot3(x, p)) / bound


def factor_kernel(
    total_tokens,
    tokens,
    out_grads,
    gradient,
    a_all,
    g_all,
    right,
    tok,
    grads,
    grad_in,
    a_part,
    a_core,
    a_ring,
    a_sum,
    a_second,
    a_line,
    a_third,
    a_cross,
    g_part,
    g_core,
    g_ring,
    g_sum,
    g_other,
    ns_in,
    full,
    state,
    load_sem,
    send_sem,
    recv_sem,
):
    dp, tensor = lax.axis_index("dp"), lax.axis_index("tensor")
    x, y_lo, c = dp // 4, (dp // 2) % 2, dp % 2
    y_hi, z = tensor // 4, tensor % 4
    y = y_hi * 2 + y_lo
    o = 1 - c

    def device(x_, y_, z_, c_):
        return {"dp": x_ * 4 + (y_ % 2) * 2 + c_, "tensor": (y_ // 2) * 4 + z_}

    def turn(position, by):
        return (position + by) % 4

    first, second = o * z + c * y, o * y + c * z

    def plane(first_, second_):
        return device(x, c * first_ + o * second_, o * first_ + c * second_, c)

    other_core = device(x, y, z, o)
    y_partner = y_hi * 2 + 1 - y_lo

    def a_core_of(y_, z_):
        return (y_ + z_ + 1) % 2

    on_a = c == a_core_of(y, z)
    on_g = jnp.logical_not(on_a)

    sent = []
    counters = {"send": 0, "recv": 0}

    def take(kind, count=1):
        at = counters[kind]
        counters[kind] += count
        return at

    def send(src, dst, recv_at, target, cond=None):
        send_at = take("send")

        def make():
            return pltpu.make_async_remote_copy(
                src_ref=src, dst_ref=dst, send_sem=send_sem.at[send_at], recv_sem=recv_sem.at[recv_at],
                device_id=target, device_id_type=MESH,
            )

        if cond is None:
            make().start()
        else:
            pl.when(cond)(lambda: make().start())
        sent.append((send_at, src.shape, cond))

    def await_recv(dst, recv_at):
        pltpu.make_async_remote_copy(
            src_ref=dst, dst_ref=dst, send_sem=send_sem.at[0], recv_sem=recv_sem.at[recv_at],
            device_id=other_core, device_id_type=MESH,
        ).wait_recv()

    def wait_sent(send_at, shape):
        like = {(ROWS, HALF): g_sum, (PIECE, HALF): a_line, (4, PIECE, HALF): a_sum}[tuple(shape)]
        pltpu.make_async_remote_copy(
            src_ref=like, dst_ref=like, send_sem=send_sem.at[send_at], recv_sem=recv_sem.at[0],
            device_id=other_core, device_id_type=MESH,
        ).wait_send()

    def finish():
        for send_at, shape, cond in sent:
            if cond is None:
                wait_sent(send_at, shape)
            else:
                pl.when(cond)(functools.partial(wait_sent, send_at, shape))

    token_load = pltpu.make_async_copy(tokens, tok, load_sem.at[8])
    token_load.start()
    gradient_load = pltpu.make_async_copy(gradient, grad_in, load_sem.at[9])

    def grad_load(at):
        i = at % 4
        core = o + (at // 4) * (c - o)
        block = 2 * turn(x, 1 + i) + (core + z) % 2
        return pltpu.make_async_copy(
            out_grads.at[:, pl.ds(pl.multiple_of(block * BLOCK, BLOCK), BLOCK)], grads.at[at], load_sem.at[at]
        )

    for at in range(8):
        grad_load(at).start()
    gradient_load.start()

    def grad_waits(stage):
        gradient_load.wait()
        for at in range(8):
            if stage == 1 or (stage <= 3 and at >= 4):
                grad_load(at).wait()

    barrier = pltpu.get_barrier_semaphore()
    others = [other_core]
    for by in (1, 2, 3):
        for core in (c, o):
            others.append(device(turn(x, by), y, z, core))
            others.append(device(x, turn(y, by), z, core))
            others.append(device(x, y, turn(z, by), core))
    for target in others:
        pl.semaphore_signal(barrier, inc=1, device_id=target, device_id_type=MESH)

    token_load.wait()

    def a_gram(k, carry):
        v = tok[:, pl.ds(pl.multiple_of(k * BLOCK, BLOCK), BLOCK)]
        pack_into(a_part.at[0, k % 4, k // 4], a_part.at[1, k // 4, k % 4], gram(v))
        return carry

    lax.fori_loop(0, 16, a_gram, 0)
    pl.semaphore_wait(barrier, len(others))

    a_core_recv = take("recv", 4)
    for i in range(4):
        at = turn(first, 1 + i)
        send(a_part.at[o, :, at], a_core.at[:, at], a_core_recv + i, other_core)

    g_core_recv = take("recv", 4)
    g_core_send = take("send", 4)

    def to_core(i):
        return pltpu.make_async_remote_copy(
            src_ref=g_part.at[i], dst_ref=g_core.at[i], send_sem=send_sem.at[g_core_send + i],
            recv_sem=recv_sem.at[g_core_recv + i], device_id=other_core, device_id_type=MESH,
        )

    def g_gram(at):
        grad_load(at).wait()
        pack_into(g_part.at[at, 0:PIECE], g_part.at[at, PIECE:ROWS], gram(grads[at]))

    def their_gram(i, carry):
        g_gram(i)
        to_core(i).start()
        return carry

    def wait_to_core(i, carry):
        to_core(i).wait_send()
        return carry

    lax.fori_loop(0, 2, their_gram, 0)

    a_ring_recv = take("recv", 12)
    for i in range(4):
        at = turn(second, 1 + i)
        await_recv(a_core.at[:, at], a_core_recv + i)
        a_part[c, :, at] += a_core[:, at]
        for by in (1, 2, 3):
            send(
                a_part.at[c, turn(first, by), at], a_ring.at[3 - by, at], a_ring_recv + 3 * i + 3 - by,
                plane(turn(first, by), second),
            )

    lax.fori_loop(2, 4, their_gram, 0)

    g_ring_recv = take("recv", 3)
    g_ring_send = take("send", 3)

    def to_x(i):
        return pltpu.make_async_remote_copy(
            src_ref=g_part.at[4 + i], dst_ref=g_ring.at[2 - i], send_sem=send_sem.at[g_ring_send + i],
            recv_sem=recv_sem.at[g_ring_recv + 2 - i], device_id=device(turn(x, 1 + i), y, z, c), device_id_type=MESH,
        )

    def my_gram(i, carry):
        g_gram(4 + i)
        await_recv(g_core.at[i], g_core_recv + i)
        g_part[4 + i] += g_core[i]

        @pl.when(i < 3)
        def _():
            to_x(i).start()

        return carry

    def wait_to_x(i, carry):
        to_x(i).wait_send()
        return carry

    lax.fori_loop(0, 4, my_gram, 0)

    a_second_recv = take("recv", 3)
    for i in range(4):
        at = turn(second, 1 + i)
        for slot in range(3):
            await_recv(a_ring.at[slot, at], a_ring_recv + 3 * i + slot)
        a_sum[i] = (a_part[c, first, at] + a_ring[0, at]) + (a_ring[1, at] + a_ring[2, at])
        if i < 3:
            send(a_sum.at[i], a_second.at[2 - i], a_second_recv + 2 - i, plane(first, at))

    for slot in range(3):
        await_recv(g_ring.at[slot], g_ring_recv + slot)
    g_sum[...] = (g_part[7] + g_ring[0]) + (g_ring[1] + g_ring[2])
    g_y_recv = take("recv")
    send(g_sum, g_other, g_y_recv, device(x, y_partner, z, c), on_a)

    for slot in range(3):
        await_recv(a_second.at[slot], a_second_recv + slot)
    a_line[...] = (a_sum[3] + a_second[0]) + (a_second[1] + a_second[2])
    a_third_recv = take("recv", 6)
    a_cross_recv = take("recv")
    for by in (1, 2, 3):
        send(
            a_line, a_third.at[3 - by, c], a_third_recv + 2 * (3 - by) + c,
            device(turn(x, by), y, z, a_core_of(y, z)),
        )
    send(a_line, a_cross, a_cross_recv, other_core, on_g)

    @pl.when(on_g)
    def _():
        await_recv(g_other, g_y_recv)
        ns_in[...] = g_sum[...] + g_other[...]

    @pl.when(on_a)
    def _():
        await_recv(a_cross, a_cross_recv)
        for slot in range(3):
            for h in range(2):
                await_recv(a_third.at[slot, h], a_third_recv + 2 * slot + h)
        here = pl.ds(pl.multiple_of(c * PIECE, 8), PIECE)
        there = pl.ds(pl.multiple_of(o * PIECE, 8), PIECE)
        ns_in[here] = (a_line[...] + a_third[0, c]) + (a_third[1, c] + a_third[2, c])
        ns_in[there] = (a_cross[...] + a_third[0, o]) + (a_third[1, o] + a_third[2, o])

    g_mine = 2 * x + y_lo
    a_mine = 4 * y + z
    unpack_into(full, ns_in[...])
    full[...] = newton_inverse(full, state, total_tokens)

    g_x_recv = take("recv", 6)
    g_p_recv = take("recv")
    g_copy_recv = take("recv", 8)
    g_sends = len(sent)

    @pl.when(on_g)
    def _():
        pack_into(g_all.at[g_mine, 0:PIECE], g_all.at[g_mine, PIECE:ROWS], full[...])
        own = g_all.at[g_mine]
        send(own, own, g_p_recv, device(x, y_partner, z, o))
        for by in (1, 2, 3):
            send(own, own, g_x_recv + 3 - by, device(turn(x, by), y, z, c))
        send(own, own, g_copy_recv + g_mine, other_core)
        beside = 2 * x + 1 - y_lo
        held = g_all.at[beside]
        await_recv(held, g_p_recv)
        for by in (1, 2, 3):
            send(held, held, g_x_recv + 3 + 3 - by, device(turn(x, by), y, z, c))
        send(held, held, g_copy_recv + beside, other_core)
        for which, low in ((0, y_lo), (1, 1 - y_lo)):
            for slot in (0, 2, 1):
                block = 2 * turn(x, 1 + slot) + low
                held = g_all.at[block]
                await_recv(held, g_x_recv + 3 * which + slot)
                send(held, held, g_copy_recv + block, other_core)

    g_sends = (g_sends, len(sent))

    a_y_recv = take("recv", 3)
    a_z_recv = take("recv", 3)
    a_top_recv = take("recv", 9)
    a_bottom_recv = take("recv", 9)
    a_copy_recv = take("recv", 16)
    a_sends = len(sent)

    def to_y(by):
        y_ = turn(y, by)
        return device(x, y_, z, a_core_of(y_, z))

    def to_z(by):
        z_ = turn(z, by)
        return device(x, y, z_, a_core_of(y, z_))

    @pl.when(on_a)
    def _():
        pack_into(a_all.at[a_mine, 0:PIECE], a_all.at[a_mine, PIECE:ROWS], full[...])
        own = a_all.at[a_mine]
        for by in (1, 3, 2):
            send(own, own, a_y_recv + 3 - by, to_y(by))
            send(own, own, a_z_recv + 3 - by, to_z(by))
        send(own, own, a_copy_recv + a_mine, other_core)
        for slot in (0, 2, 1):
            block = 4 * turn(y, 1 + slot) + z
            await_recv(a_all.at[block], a_y_recv + slot)
            top = a_all.at[block, 0:PIECE]
            for by in (1, 3, 2):
                send(top, top, a_top_recv + 3 * slot + 3 - by, to_z(by))
            send(a_all.at[block], a_all.at[block], a_copy_recv + block, other_core)
            block = 4 * y + turn(z, 1 + slot)
            await_recv(a_all.at[block], a_z_recv + slot)
            bottom = a_all.at[block, PIECE:ROWS]
            for by in (1, 3, 2):
                send(bottom, bottom, a_bottom_recv + 3 * slot + 3 - by, to_y(by))
            send(a_all.at[block], a_all.at[block], a_copy_recv + block, other_core)

        def copied(block, carry):
            await_recv(g_all.at[block], g_copy_recv + block)
            return carry

        lax.fori_loop(0, 8, copied, 0)

    gradient_load.wait()

    def right_product(j, carry):
        columns = pl.ds(pl.multiple_of(j * BLOCK, BLOCK), BLOCK)
        unpack_into(full, g_all[j])
        right[:, columns] = dot3(grad_in[:, columns], full[...])
        return carry

    lax.fori_loop(0, 8, right_product, 0)

    @pl.when(on_a)
    def _():
        for slot_y in (0, 2, 1):
            for slot_z in (0, 2, 1):
                block = 4 * turn(y, 1 + slot_y) + turn(z, 1 + slot_z)
                await_recv(a_all.at[block, 0:PIECE], a_top_recv + 3 * slot_y + slot_z)
                await_recv(a_all.at[block, PIECE:ROWS], a_bottom_recv + 3 * slot_z + slot_y)
                send(a_all.at[block], a_all.at[block], a_copy_recv + block, other_core)

    a_sends = (a_sends, len(sent))

    @pl.when(on_g)
    def _():
        def copied(block, carry):
            await_recv(a_all.at[block], a_copy_recv + block)
            return carry

        lax.fori_loop(0, 16, copied, 0)

    for (start, stop), held_here in ((g_sends, on_g), (a_sends, on_a)):
        for index in range(start, stop):
            sent[index] = (*sent[index][:2], held_here)
    lax.fori_loop(0, 4, wait_to_core, 0)
    lax.fori_loop(0, 3, wait_to_x, 0)
    finish()


def factors(tokens, out_grads, gradient, total_tokens):
    vmem = pl.BlockSpec(memory_space=pltpu.VMEM)
    anywhere = pl.BlockSpec(memory_space=pltpu.HBM)

    def pieces(*lead):
        return pltpu.VMEM((*lead, PIECE, HALF), F32)

    def blocks(*lead):
        return pltpu.VMEM((*lead, ROWS, HALF), F32)

    return pl.pallas_call(
        functools.partial(factor_kernel, total_tokens),
        out_shape=(
            jax.ShapeDtypeStruct((16, ROWS, HALF), F32),
            jax.ShapeDtypeStruct((8, ROWS, HALF), F32),
            jax.ShapeDtypeStruct(gradient.shape, F32),
        ),
        in_specs=[anywhere, anywhere, anywhere],
        out_specs=(vmem, vmem, vmem),
        scratch_shapes=[
            pltpu.VMEM(tokens.shape, BF16),
            pltpu.VMEM((8, 2048, BLOCK), BF16),
            pltpu.VMEM(gradient.shape, F32),
            pieces(2, 4, 4),
            pieces(4, 4),
            pieces(3, 4),
            pieces(4),
            pieces(3),
            pieces(),
            pieces(3, 2),
            pieces(),
            blocks(8),
            blocks(4),
            blocks(3),
            blocks(),
            blocks(),
            blocks(),
            pltpu.VMEM((BLOCK, BLOCK), F32),
            pltpu.VMEM((2 * BLOCK, BLOCK), F32),
            pltpu.SemaphoreType.DMA((10,)),
            pltpu.SemaphoreType.DMA((128,)),
            pltpu.SemaphoreType.DMA((128,)),
        ],
        compiler_params=pltpu.CompilerParams(
            collective_id=0, has_side_effects=True, vmem_limit_bytes=48 * 2**20
        ),
        name="factors",
    )(tokens, out_grads, gradient)


def apply_kernel(owners, a_all, g_all, right, out, inverses, left, result, placed, out_sem):
    dp = lax.axis_index("dp")
    width = right.shape[1] // 4
    unpack_into(left, a_all[dp])

    def out_copy(q):
        columns = pl.ds(pl.multiple_of(q * width, width), width)
        return pltpu.make_async_copy(result.at[:, columns], out.at[:, columns], out_sem.at[q])

    def left_product(q, carry):
        columns = pl.ds(pl.multiple_of(q * width, width), width)
        result[:, columns] = dot3(left[...], right[:, columns])
        out_copy(q).start()
        return carry

    lax.fori_loop(0, 4, left_product, 0)

    def scan(b, carry):
        seen, slots = carry
        hit = owners[0, b] == dp
        slots = tuple(jnp.where(jnp.logical_and(hit, seen == s), b, slot) for s, slot in enumerate(slots))
        return seen + hit.astype(jnp.int32), slots

    _, slots = lax.fori_loop(0, 24, scan, (jnp.int32(0), (jnp.int32(-1),) * 3))
    for s, chosen in enumerate(slots):
        @pl.when(chosen < 0)
        def _():
            placed[s] = jnp.zeros((BLOCK, BLOCK), F32)

        @pl.when(jnp.logical_and(chosen >= 0, chosen < 16))
        def _():
            unpack_into(placed.at[s], a_all[chosen])

        @pl.when(chosen >= 16)
        def _():
            unpack_into(placed.at[s], g_all[chosen - 16])

        pltpu.make_async_copy(placed.at[s], inverses.at[0, 0, s], out_sem.at[4 + s]).start()
    for q in range(4):
        out_copy(q).wait()
    for s in range(3):
        pltpu.make_async_copy(placed.at[s], inverses.at[0, 0, s], out_sem.at[4 + s]).wait()


def apply(owners, a_all, g_all, right):
    vmem = pl.BlockSpec(memory_space=pltpu.VMEM)
    anywhere = pl.BlockSpec(memory_space=pl.ANY)
    return pl.pallas_call(
        apply_kernel,
        out_shape=(
            jax.ShapeDtypeStruct(right.shape, F32),
            jax.ShapeDtypeStruct((1, 1, 3, BLOCK, BLOCK), F32),
        ),
        in_specs=[pl.BlockSpec(memory_space=pltpu.SMEM), vmem, vmem, vmem],
        out_specs=(anywhere, anywhere),
        scratch_shapes=[
            pltpu.VMEM((BLOCK, BLOCK), F32),
            pltpu.VMEM(right.shape, F32),
            pltpu.VMEM((3, BLOCK, BLOCK), F32),
            pltpu.SemaphoreType.DMA((7,)),
        ],
        compiler_params=pltpu.CompilerParams(vmem_limit_bytes=32 * 2**20),
        name="apply",
    )(owners, a_all, g_all, right)


def on_device(tokens, out_grads, gradient, owners):
    total_tokens = tokens.shape[0] * lax.axis_size("tensor") * lax.axis_size("dp")
    a_all, g_all, right = factors(tokens, out_grads, gradient, total_tokens)
    return apply(owners, a_all, g_all, right)


def solution(mesh):
    placed = (P(("dp", "tensor"), None), P("dp", "tensor"), P("dp", "tensor"), P("tensor", None))
    return jax.shard_map(
        on_device,
        mesh=mesh,
        in_specs=placed,
        out_specs=(P("dp", "tensor"), P("tensor", "dp", None, None, None)),
        check_vma=False,
    )
```

```python
import functools
import jax
import jax.numpy as jnp
from jax import lax
from jax.experimental import pallas as pl
from jax.experimental.pallas import tpu as pltpu
from jax.sharding import PartitionSpec as P

BLOCK = 256
HALF = 128
PIECE = 136
ROWS = 2 * PIECE
NS_ITERS = 12
DAMPING = 0.01
MESH = pl.DeviceIdType.MESH
F32 = jnp.float32
BF16 = jnp.bfloat16


def iotas(n):
    return (
        lax.broadcasted_iota(jnp.int32, (n, n), 0),
        lax.broadcasted_iota(jnp.int32, (n, n), 1),
    )


def pack_into(top, bottom, full):
    row, col = iotas(HALF)
    upper_left, lower_right = full[:HALF, :HALF], full[HALF:, HALF:]
    top[0:HALF, :] = jnp.where(row >= col, upper_left, lower_right)
    diagonal = jnp.sum(jnp.where(row == col, lower_right, 0.0), axis=0, keepdims=True)
    top[HALF:PIECE, :] = jnp.broadcast_to(diagonal, (PIECE - HALF, HALF))
    bottom[0:HALF, :] = full[HALF:, :HALF]
    bottom[HALF:PIECE, :] = jnp.zeros((PIECE - HALF, HALF), F32)


def unpack_into(dst, packed):
    row, col = iotas(HALF)
    both, below = packed[0:HALF, :], packed[PIECE:PIECE + HALF, :]
    diagonal = packed[HALF:HALF + 1, :]
    turned = both.T
    dst[0:HALF, 0:HALF] = jnp.where(row >= col, both, turned)
    dst[HALF:BLOCK, HALF:BLOCK] = jnp.where(row < col, both, jnp.where(row == col, diagonal, turned))
    dst[HALF:BLOCK, 0:HALF] = below
    dst[0:HALF, HALF:BLOCK] = below.T


def bdot(a, b):
    return jnp.dot(a, b, preferred_element_type=F32)


def gram(v):
    return lax.dot_general(v, v, (((0,), (0,)), ((), ())), preferred_element_type=F32)


def split2(v):
    high = v.astype(BF16)
    return high, (v - high.astype(F32)).astype(BF16)


def split3(v):
    high = v.astype(BF16)
    rest = v - high.astype(F32)
    mid = rest.astype(BF16)
    return high, mid, (rest - mid.astype(F32)).astype(BF16)


def dot3(a, b):
    ah, al = split2(a)
    bh, bl = split2(b)
    return (bdot(ah, bl) + bdot(al, bh)) + bdot(ah, bh)


def newton_inverse(full, state, total_tokens):
    row, col = iotas(BLOCK)
    on_diagonal = row == col
    cov = full[...] * (1.0 / total_tokens)
    trace = jnp.sum(jnp.where(on_diagonal, cov, 0.0))
    damped = cov + jnp.where(on_diagonal, DAMPING / BLOCK * trace, 0.0)
    bound = jnp.max(jnp.sum(jnp.abs(damped), axis=0, keepdims=True), axis=1, keepdims=True)
    p = damped / bound
    state[BLOCK:, :] = jnp.where(on_diagonal, 2.0, 0.0) - p
    state[:BLOCK, :] = 2.0 * p - jnp.dot(p, p, precision=lax.Precision.HIGHEST)

    def sweep(index, carry):
        p, x = state[:BLOCK, :], state[BLOCK:, :]
        ph, pm, pl_ = split3(p)
        xh, xm = split2(x)
        by_high = bdot(jnp.concatenate([pl_, pm, ph, xm, xh], 0), ph)
        by_mid = bdot(jnp.concatenate([pm, ph, xh], 0), pm)
        by_low = bdot(ph, pl_)
        n = BLOCK
        pp = ((by_low + by_high[:n] + by_mid[:n]) + (by_high[n:2 * n] + by_mid[n:2 * n])) + by_high[2 * n:3 * n]
        xp = (by_high[3 * n:4 * n] + by_mid[2 * n:]) + by_high[4 * n:]
        state[:BLOCK, :] = 2.0 * p - pp
        state[BLOCK:, :] = 2.0 * x - xp
        return carry

    lax.fori_loop(0, NS_ITERS - 2, sweep, 0)
    p, x = state[:BLOCK, :], state[BLOCK:, :]
    return (2.0 * x - dot3(x, p)) / bound


def factor_kernel(
    total_tokens,
    tokens,
    out_grads,
    gradient,
    a_all,
    g_all,
    right,
    tok,
    grads,
    grad_in,
    a_part,
    a_core,
    a_ring,
    a_sum,
    a_second,
    a_line,
    a_third,
    a_cross,
    g_part,
    g_core,
    g_ring,
    g_sum,
    g_other,
    ns_in,
    full,
    state,
    load_sem,
    send_sem,
    recv_sem,
):
    dp, tensor = lax.axis_index("dp"), lax.axis_index("tensor")
    x, y_lo, c = dp // 4, (dp // 2) % 2, dp % 2
    y_hi, z = tensor // 4, tensor % 4
    y = y_hi * 2 + y_lo
    o = 1 - c

    def device(x_, y_, z_, c_):
        return {"dp": x_ * 4 + (y_ % 2) * 2 + c_, "tensor": (y_ // 2) * 4 + z_}

    def turn(position, by):
        return (position + by) % 4

    first, second = o * z + c * y, o * y + c * z

    def plane(first_, second_):
        return device(x, c * first_ + o * second_, o * first_ + c * second_, c)

    other_core = device(x, y, z, o)
    y_partner = y_hi * 2 + 1 - y_lo

    def a_core_of(y_, z_):
        return (y_ + z_ + 1) % 2

    on_a = c == a_core_of(y, z)
    on_g = jnp.logical_not(on_a)

    sent = []
    counters = {"send": 0, "recv": 0}

    def take(kind, count=1):
        at = counters[kind]
        counters[kind] += count
        return at

    def send(src, dst, recv_at, target, cond=None):
        send_at = take("send")

        def make():
            return pltpu.make_async_remote_copy(
                src_ref=src, dst_ref=dst, send_sem=send_sem.at[send_at], recv_sem=recv_sem.at[recv_at],
                device_id=target, device_id_type=MESH,
            )

        if cond is None:
            make().start()
        else:
            pl.when(cond)(lambda: make().start())
        sent.append((send_at, src.shape, cond))

    def await_recv(dst, recv_at):
        pltpu.make_async_remote_copy(
            src_ref=dst, dst_ref=dst, send_sem=send_sem.at[0], recv_sem=recv_sem.at[recv_at],
            device_id=other_core, device_id_type=MESH,
        ).wait_recv()

    def wait_sent(send_at, shape):
        like = {(ROWS, HALF): g_sum, (PIECE, HALF): a_line, (4, PIECE, HALF): a_sum}[tuple(shape)]
        pltpu.make_async_remote_copy(
            src_ref=like, dst_ref=like, send_sem=send_sem.at[send_at], recv_sem=recv_sem.at[0],
            device_id=other_core, device_id_type=MESH,
        ).wait_send()

    def finish():
        for send_at, shape, cond in sent:
            if cond is None:
                wait_sent(send_at, shape)
            else:
                pl.when(cond)(functools.partial(wait_sent, send_at, shape))

    barrier = pltpu.get_barrier_semaphore()
    others = [other_core]
    for by in (1, 2, 3):
        for core in (c, o):
            others.append(device(turn(x, by), y, z, core))
            others.append(device(x, turn(y, by), z, core))
            others.append(device(x, y, turn(z, by), core))
    for target in others:
        pl.semaphore_signal(barrier, inc=1, device_id=target, device_id_type=MESH)

    token_load = pltpu.make_async_copy(tokens, tok, load_sem.at[8])
    token_load.start()
    gradient_load = pltpu.make_async_copy(gradient, grad_in, load_sem.at[9])

    def grad_load(at):
        i = at % 4
        core = o + (at // 4) * (c - o)
        block = 2 * turn(x, 1 + i) + (core + z) % 2
        return pltpu.make_async_copy(
            out_grads.at[:, pl.ds(pl.multiple_of(block * BLOCK, BLOCK), BLOCK)], grads.at[at], load_sem.at[at]
        )

    for at in range(8):
        grad_load(at).start()
    gradient_load.start()

    def grad_waits(stage):
        gradient_load.wait()
        for at in range(8):
            if stage == 1 or (stage <= 3 and at >= 4):
                grad_load(at).wait()

    token_load.wait()

    def a_gram(k, carry):
        v = tok[:, pl.ds(pl.multiple_of(k * BLOCK, BLOCK), BLOCK)]
        pack_into(a_part.at[0, k % 4, k // 4], a_part.at[1, k // 4, k % 4], gram(v))
        return carry

    lax.fori_loop(0, 16, a_gram, 0, unroll=4)
    pl.semaphore_wait(barrier, len(others))

    a_core_recv = take("recv", 4)
    for i in range(4):
        at = turn(first, 1 + i)
        send(a_part.at[o, :, at], a_core.at[:, at], a_core_recv + i, other_core)

    g_core_recv = take("recv", 4)
    g_core_send = take("send", 4)

    def to_core(i):
        return pltpu.make_async_remote_copy(
            src_ref=g_part.at[i], dst_ref=g_core.at[i], send_sem=send_sem.at[g_core_send + i],
            recv_sem=recv_sem.at[g_core_recv + i], device_id=other_core, device_id_type=MESH,
        )

    def g_gram(at):
        grad_load(at).wait()
        pack_into(g_part.at[at, 0:PIECE], g_part.at[at, PIECE:ROWS], gram(grads[at]))

    def their_gram(i, carry):
        g_gram(i)
        to_core(i).start()
        return carry

    def wait_to_core(i, carry):
        to_core(i).wait_send()
        return carry

    lax.fori_loop(0, 2, their_gram, 0, unroll=2)

    a_ring_recv = take("recv", 12)
    for i in range(4):
        at = turn(second, 1 + i)
        await_recv(a_core.at[:, at], a_core_recv + i)
        a_part[c, :, at] += a_core[:, at]
        for by in (1, 2, 3):
            send(
                a_part.at[c, turn(first, by), at], a_ring.at[3 - by, at], a_ring_recv + 3 * i + 3 - by,
                plane(turn(first, by), second),
            )

    lax.fori_loop(2, 4, their_gram, 0, unroll=2)

    g_ring_recv = take("recv", 3)
    g_ring_send = take("send", 3)

    def to_x(i):
        return pltpu.make_async_remote_copy(
            src_ref=g_part.at[4 + i], dst_ref=g_ring.at[2 - i], send_sem=send_sem.at[g_ring_send + i],
            recv_sem=recv_sem.at[g_ring_recv + 2 - i], device_id=device(turn(x, 1 + i), y, z, c), device_id_type=MESH,
        )

    def my_gram(i, carry):
        g_gram(4 + i)
        await_recv(g_core.at[i], g_core_recv + i)
        g_part[4 + i] += g_core[i]

        @pl.when(i < 3)
        def _():
            to_x(i).start()

        return carry

    def wait_to_x(i, carry):
        to_x(i).wait_send()
        return carry

    lax.fori_loop(0, 4, my_gram, 0, unroll=2)

    a_second_recv = take("recv", 3)
    for i in range(4):
        at = turn(second, 1 + i)
        for slot in range(3):
            await_recv(a_ring.at[slot, at], a_ring_recv + 3 * i + slot)
        a_sum[i] = (a_part[c, first, at] + a_ring[0, at]) + (a_ring[1, at] + a_ring[2, at])
        if i < 3:
            send(a_sum.at[i], a_second.at[2 - i], a_second_recv + 2 - i, plane(first, at))

    for slot in range(3):
        await_recv(g_ring.at[slot], g_ring_recv + slot)
    g_sum[...] = (g_part[7] + g_ring[0]) + (g_ring[1] + g_ring[2])
    g_y_recv = take("recv")
    send(g_sum, g_other, g_y_recv, device(x, y_partner, z, c), on_a)

    for slot in range(3):
        await_recv(a_second.at[slot], a_second_recv + slot)
    a_line[...] = (a_sum[3] + a_second[0]) + (a_second[1] + a_second[2])
    a_third_recv = take("recv", 6)
    a_cross_recv = take("recv")
    for by in (1, 2, 3):
        send(
            a_line, a_third.at[3 - by, c], a_third_recv + 2 * (3 - by) + c,
            device(turn(x, by), y, z, a_core_of(y, z)),
        )
    send(a_line, a_cross, a_cross_recv, other_core, on_g)

    @pl.when(on_g)
    def _():
        await_recv(g_other, g_y_recv)
        ns_in[...] = g_sum[...] + g_other[...]

    @pl.when(on_a)
    def _():
        await_recv(a_cross, a_cross_recv)
        for slot in range(3):
            for h in range(2):
                await_recv(a_third.at[slot, h], a_third_recv + 2 * slot + h)
        here = pl.ds(pl.multiple_of(c * PIECE, 8), PIECE)
        there = pl.ds(pl.multiple_of(o * PIECE, 8), PIECE)
        ns_in[here] = (a_line[...] + a_third[0, c]) + (a_third[1, c] + a_third[2, c])
        ns_in[there] = (a_cross[...] + a_third[0, o]) + (a_third[1, o] + a_third[2, o])

    g_mine = 2 * x + y_lo
    a_mine = 4 * y + z
    unpack_into(full, ns_in[...])
    full[...] = newton_inverse(full, state, total_tokens)

    g_x_recv = take("recv", 6)
    g_p_recv = take("recv")
    g_copy_recv = take("recv", 8)
    g_sends = len(sent)

    @pl.when(on_g)
    def _():
        pack_into(g_all.at[g_mine, 0:PIECE], g_all.at[g_mine, PIECE:ROWS], full[...])
        own = g_all.at[g_mine]
        send(own, own, g_p_recv, device(x, y_partner, z, o))
        for by in (1, 2, 3):
            send(own, own, g_x_recv + 3 - by, device(turn(x, by), y, z, c))
        send(own, own, g_copy_recv + g_mine, other_core)
        beside = 2 * x + 1 - y_lo
        held = g_all.at[beside]
        await_recv(held, g_p_recv)
        for by in (1, 2, 3):
            send(held, held, g_x_recv + 3 + 3 - by, device(turn(x, by), y, z, c))
        send(held, held, g_copy_recv + beside, other_core)
        for which, low in ((0, y_lo), (1, 1 - y_lo)):
            for slot in (0, 2, 1):
                block = 2 * turn(x, 1 + slot) + low
                held = g_all.at[block]
                await_recv(held, g_x_recv + 3 * which + slot)
                send(held, held, g_copy_recv + block, other_core)

    g_sends = (g_sends, len(sent))

    a_y_recv = take("recv", 6)
    a_z_recv = take("recv", 6)
    a_top_recv = take("recv", 9)
    a_bottom_recv = take("recv", 9)
    a_copy_recv = take("recv", 16)
    a_sends = len(sent)

    def to_y(by):
        y_ = turn(y, by)
        return device(x, y_, z, a_core_of(y_, z))

    def to_z(by):
        z_ = turn(z, by)
        return device(x, y, z_, a_core_of(y, z_))

    @pl.when(on_a)
    def _():
        pack_into(a_all.at[a_mine, 0:PIECE], a_all.at[a_mine, PIECE:ROWS], full[...])
        own = a_all.at[a_mine]
        own_top, own_bottom = a_all.at[a_mine, 0:PIECE], a_all.at[a_mine, PIECE:ROWS]
        for by in (1, 3, 2):
            send(own_top, own_top, a_y_recv + 3 - by, to_y(by))
            send(own_bottom, own_bottom, a_z_recv + 3 - by, to_z(by))
        for by in (1, 3, 2):
            send(own_bottom, own_bottom, a_y_recv + 6 - by, to_y(by))
            send(own_top, own_top, a_z_recv + 6 - by, to_z(by))
        send(own, own, a_copy_recv + a_mine, other_core)
        for slot in (0, 2, 1):
            top = a_all.at[4 * turn(y, 1 + slot) + z, 0:PIECE]
            await_recv(top, a_y_recv + slot)
            for by in (1, 3, 2):
                send(top, top, a_top_recv + 3 * slot + 3 - by, to_z(by))
            bottom = a_all.at[4 * y + turn(z, 1 + slot), PIECE:ROWS]
            await_recv(bottom, a_z_recv + slot)
            for by in (1, 3, 2):
                send(bottom, bottom, a_bottom_recv + 3 * slot + 3 - by, to_y(by))
        for slot in (0, 2, 1):
            block = 4 * turn(y, 1 + slot) + z
            await_recv(a_all.at[block, PIECE:ROWS], a_y_recv + 3 + slot)
            send(a_all.at[block], a_all.at[block], a_copy_recv + block, other_core)
            block = 4 * y + turn(z, 1 + slot)
            await_recv(a_all.at[block, 0:PIECE], a_z_recv + 3 + slot)
            send(a_all.at[block], a_all.at[block], a_copy_recv + block, other_core)

        def copied(block, carry):
            await_recv(g_all.at[block], g_copy_recv + block)
            return carry

        lax.fori_loop(0, 8, copied, 0)

    gradient_load.wait()

    def right_product(j, carry):
        columns = pl.ds(pl.multiple_of(j * BLOCK, BLOCK), BLOCK)
        unpack_into(full, g_all[j])
        right[:, columns] = dot3(grad_in[:, columns], full[...])
        return carry

    lax.fori_loop(0, 8, right_product, 0, unroll=4)

    @pl.when(on_a)
    def _():
        for slot_y in (0, 2, 1):
            for slot_z in (0, 2, 1):
                block = 4 * turn(y, 1 + slot_y) + turn(z, 1 + slot_z)
                await_recv(a_all.at[block, 0:PIECE], a_top_recv + 3 * slot_y + slot_z)
                await_recv(a_all.at[block, PIECE:ROWS], a_bottom_recv + 3 * slot_z + slot_y)
                send(a_all.at[block], a_all.at[block], a_copy_recv + block, other_core)

    a_sends = (a_sends, len(sent))

    @pl.when(on_g)
    def _():
        def copied(block, carry):
            await_recv(a_all.at[block], a_copy_recv + block)
            return carry

        lax.fori_loop(0, 16, copied, 0)

    for (start, stop), held_here in ((g_sends, on_g), (a_sends, on_a)):
        for index in range(start, stop):
            sent[index] = (*sent[index][:2], held_here)
    lax.fori_loop(0, 4, wait_to_core, 0)
    lax.fori_loop(0, 3, wait_to_x, 0)
    finish()


def factors(tokens, out_grads, gradient, total_tokens):
    vmem = pl.BlockSpec(memory_space=pltpu.VMEM)
    anywhere = pl.BlockSpec(memory_space=pltpu.HBM)

    def pieces(*lead):
        return pltpu.VMEM((*lead, PIECE, HALF), F32)

    def blocks(*lead):
        return pltpu.VMEM((*lead, ROWS, HALF), F32)

    tokens, out_grads, gradient = (
        pltpu.with_memory_space_constraint(v, pltpu.HBM) for v in (tokens, out_grads, gradient)
    )
    return pl.pallas_call(
        functools.partial(factor_kernel, total_tokens),
        out_shape=(
            jax.ShapeDtypeStruct((16, ROWS, HALF), F32),
            jax.ShapeDtypeStruct((8, ROWS, HALF), F32),
            jax.ShapeDtypeStruct(gradient.shape, F32),
        ),
        in_specs=[anywhere, anywhere, anywhere],
        out_specs=(vmem, vmem, vmem),
        scratch_shapes=[
            pltpu.VMEM(tokens.shape, BF16),
            pltpu.VMEM((8, 2048, BLOCK), BF16),
            pltpu.VMEM(gradient.shape, F32),
            pieces(2, 4, 4),
            pieces(4, 4),
            pieces(3, 4),
            pieces(4),
            pieces(3),
            pieces(),
            pieces(3, 2),
            pieces(),
            blocks(8),
            blocks(4),
            blocks(3),
            blocks(),
            blocks(),
            blocks(),
            pltpu.VMEM((BLOCK, BLOCK), F32),
            pltpu.VMEM((2 * BLOCK, BLOCK), F32),
            pltpu.SemaphoreType.DMA((10,)),
            pltpu.SemaphoreType.DMA((128,)),
            pltpu.SemaphoreType.DMA((128,)),
        ],
        compiler_params=pltpu.CompilerParams(
            collective_id=0, has_side_effects=True, vmem_limit_bytes=32 * 2**20
        ),
        name="factors",
    )(tokens, out_grads, gradient)


def apply_kernel(owners, a_all, g_all, right, out, inverses, left, result, placed, out_sem):
    dp = lax.axis_index("dp")
    width = right.shape[1] // 4
    unpack_into(left, a_all[dp])

    def out_copy(q):
        columns = pl.ds(pl.multiple_of(q * width, width), width)
        return pltpu.make_async_copy(result.at[:, columns], out.at[:, columns], out_sem.at[q])

    def left_product(q, carry):
        columns = pl.ds(pl.multiple_of(q * width, width), width)
        result[:, columns] = dot3(left[...], right[:, columns])
        out_copy(q).start()
        return carry

    lax.fori_loop(0, 4, left_product, 0, unroll=2)

    def scan(b, carry):
        seen, slots = carry
        hit = owners[0, b] == dp
        slots = tuple(jnp.where(jnp.logical_and(hit, seen == s), b, slot) for s, slot in enumerate(slots))
        return seen + hit.astype(jnp.int32), slots

    _, slots = lax.fori_loop(0, 24, scan, (jnp.int32(0), (jnp.int32(-1),) * 3))
    for s, chosen in enumerate(slots):
        @pl.when(chosen < 0)
        def _():
            placed[s] = jnp.zeros((BLOCK, BLOCK), F32)

        @pl.when(jnp.logical_and(chosen >= 0, chosen < 16))
        def _():
            unpack_into(placed.at[s], a_all[chosen])

        @pl.when(chosen >= 16)
        def _():
            unpack_into(placed.at[s], g_all[chosen - 16])

        pltpu.make_async_copy(placed.at[s], inverses.at[0, 0, s], out_sem.at[4 + s]).start()
    for q in range(4):
        out_copy(q).wait()
    for s in range(3):
        pltpu.make_async_copy(placed.at[s], inverses.at[0, 0, s], out_sem.at[4 + s]).wait()


def apply(owners, a_all, g_all, right):
    vmem = pl.BlockSpec(memory_space=pltpu.VMEM)
    anywhere = pl.BlockSpec(memory_space=pl.ANY)
    return pl.pallas_call(
        apply_kernel,
        out_shape=(
            jax.ShapeDtypeStruct(right.shape, F32),
            jax.ShapeDtypeStruct((1, 1, 3, BLOCK, BLOCK), F32),
        ),
        in_specs=[pl.BlockSpec(memory_space=pltpu.SMEM), vmem, vmem, vmem],
        out_specs=(anywhere, anywhere),
        scratch_shapes=[
            pltpu.VMEM((BLOCK, BLOCK), F32),
            pltpu.VMEM(right.shape, F32),
            pltpu.VMEM((3, BLOCK, BLOCK), F32),
            pltpu.SemaphoreType.DMA((7,)),
        ],
        compiler_params=pltpu.CompilerParams(vmem_limit_bytes=32 * 2**20),
        name="apply",
    )(owners, a_all, g_all, right)


def on_device(tokens, out_grads, gradient, owners):
    total_tokens = tokens.shape[0] * lax.axis_size("tensor") * lax.axis_size("dp")
    a_all, g_all, right = factors(tokens, out_grads, gradient, total_tokens)
    return apply(owners, a_all, g_all, right)


def solution(mesh):
    placed = (P(("dp", "tensor"), None), P("dp", "tensor"), P("dp", "tensor"), P("tensor", None))
    return jax.shard_map(
        on_device,
        mesh=mesh,
        in_specs=placed,
        out_specs=(P("dp", "tensor"), P("tensor", "dp", None, None, None)),
        check_vma=False,
    )
```

```python
import functools
import jax
import jax.numpy as jnp
from jax import lax
from jax.experimental import pallas as pl
from jax.experimental.pallas import tpu as pltpu
from jax.sharding import PartitionSpec as P

BLOCK = 256
HALF = 128
PIECE = 136
ROWS = 2 * PIECE
GROUP = 32
TOP = 3 * GROUP + 8
CODED = TOP + 3 * GROUP
NS_ITERS = 12
DAMPING = 0.01
MESH = pl.DeviceIdType.MESH
F32 = jnp.float32
BF16 = jnp.bfloat16


def iotas(n):
    return (
        lax.broadcasted_iota(jnp.int32, (n, n), 0),
        lax.broadcasted_iota(jnp.int32, (n, n), 1),
    )


def pack_into(top, bottom, full):
    row, col = iotas(HALF)
    upper_left, lower_right = full[:HALF, :HALF], full[HALF:, HALF:]
    top[0:HALF, :] = jnp.where(row >= col, upper_left, lower_right)
    diagonal = jnp.sum(jnp.where(row == col, lower_right, 0.0), axis=0, keepdims=True)
    top[HALF:PIECE, :] = jnp.broadcast_to(diagonal, (PIECE - HALF, HALF))
    bottom[0:HALF, :] = full[HALF:, :HALF]
    bottom[HALF:PIECE, :] = jnp.zeros((PIECE - HALF, HALF), F32)


def unpack_into(dst, packed):
    row, col = iotas(HALF)
    both, below = packed[0:HALF, :], packed[PIECE:PIECE + HALF, :]
    diagonal = packed[HALF:HALF + 1, :]
    turned = both.T
    dst[0:HALF, 0:HALF] = jnp.where(row >= col, both, turned)
    dst[HALF:BLOCK, HALF:BLOCK] = jnp.where(row < col, both, jnp.where(row == col, diagonal, turned))
    dst[HALF:BLOCK, 0:HALF] = below
    dst[0:HALF, HALF:BLOCK] = below.T


def to_words(v):
    first, second, third, fourth = (v[k * GROUP:(k + 1) * GROUP] for k in range(4))
    return (
        (first & 0xFFFFFF) | (fourth << 24),
        (second & 0xFFFFFF) | ((fourth >> 8) << 24),
        (third & 0xFFFFFF) | ((fourth >> 16) << 24),
    )


def from_words(words):
    parts = [words[k * GROUP:(k + 1) * GROUP] for k in range(3)]
    low, mid, high = parts
    fourth = ((low >> 24) & 0xFF) | (((mid >> 24) & 0xFF) << 8) | ((high >> 24) << 16)
    return jnp.concatenate([(w << 8) >> 8 for w in parts] + [fourth], axis=0)


def encode_into(dst, full):
    row, col = iotas(HALF)
    peak = jnp.max(jnp.max(jnp.abs(full), axis=0, keepdims=True), axis=1, keepdims=True)
    exponent = jnp.floor(jnp.log2(peak) + 1.01)
    scaled = full * (8388608.0 / jnp.exp2(exponent))
    whole = (scaled + jnp.where(scaled >= 0.0, 0.5, -0.5)).astype(jnp.int32)
    upper_left, lower_right = whole[:HALF, :HALF], whole[HALF:, HALF:]
    for k, words in enumerate(to_words(jnp.where(row >= col, upper_left, lower_right))):
        dst[k * GROUP:(k + 1) * GROUP, :] = words
    diagonal = jnp.sum(jnp.where(row == col, lower_right, 0), axis=0, keepdims=True)
    tile_row = lax.broadcasted_iota(jnp.int32, (8, HALF), 0)
    dst[3 * GROUP:TOP, :] = jnp.where(tile_row == 0, diagonal, exponent.astype(jnp.int32))
    for k, words in enumerate(to_words(whole[HALF:, :HALF])):
        dst[TOP + k * GROUP:TOP + (k + 1) * GROUP, :] = words


def decode_into(dst, coded):
    row, col = iotas(HALF)
    scale = jnp.exp2(coded[3 * GROUP + 1:3 * GROUP + 2, :].astype(F32)) * (1.0 / 8388608.0)
    both = from_words(coded[:3 * GROUP]).astype(F32) * scale
    diagonal = coded[3 * GROUP:3 * GROUP + 1, :].astype(F32) * scale
    below = from_words(coded[TOP:]).astype(F32) * scale
    turned = both.T
    dst[0:HALF, 0:HALF] = jnp.where(row >= col, both, turned)
    dst[HALF:BLOCK, HALF:BLOCK] = jnp.where(row < col, both, jnp.where(row == col, diagonal, turned))
    dst[HALF:BLOCK, 0:HALF] = below
    dst[0:HALF, HALF:BLOCK] = below.T


def bdot(a, b):
    return jnp.dot(a, b, preferred_element_type=F32)


def gram(v):
    return lax.dot_general(v, v, (((0,), (0,)), ((), ())), preferred_element_type=F32)


def split2(v):
    high = v.astype(BF16)
    return high, (v - high.astype(F32)).astype(BF16)


def split3(v):
    high = v.astype(BF16)
    rest = v - high.astype(F32)
    mid = rest.astype(BF16)
    return high, mid, (rest - mid.astype(F32)).astype(BF16)


def dot3(a, b):
    ah, al = split2(a)
    bh, bl = split2(b)
    return (bdot(ah, bl) + bdot(al, bh)) + bdot(ah, bh)


def newton_inverse(full, state, total_tokens):
    row, col = iotas(BLOCK)
    on_diagonal = row == col
    cov = full[...] * (1.0 / total_tokens)
    trace = jnp.sum(jnp.where(on_diagonal, cov, 0.0))
    damped = cov + jnp.where(on_diagonal, DAMPING / BLOCK * trace, 0.0)
    bound = jnp.max(jnp.sum(jnp.abs(damped), axis=0, keepdims=True), axis=1, keepdims=True)
    p = damped / bound
    state[BLOCK:, :] = jnp.where(on_diagonal, 2.0, 0.0) - p
    state[:BLOCK, :] = 2.0 * p - jnp.dot(p, p, precision=lax.Precision.HIGHEST)

    def sweep(index, carry):
        p, x = state[:BLOCK, :], state[BLOCK:, :]
        ph, pm, pl_ = split3(p)
        xh, xm = split2(x)
        by_high = bdot(jnp.concatenate([pl_, pm, ph, xm, xh], 0), ph)
        by_mid = bdot(jnp.concatenate([pm, ph, xh], 0), pm)
        by_low = bdot(ph, pl_)
        n = BLOCK
        pp = ((by_low + by_high[:n] + by_mid[:n]) + (by_high[n:2 * n] + by_mid[n:2 * n])) + by_high[2 * n:3 * n]
        xp = (by_high[3 * n:4 * n] + by_mid[2 * n:]) + by_high[4 * n:]
        state[:BLOCK, :] = 2.0 * p - pp
        state[BLOCK:, :] = 2.0 * x - xp
        return carry

    lax.fori_loop(0, NS_ITERS - 2, sweep, 0)
    p, x = state[:BLOCK, :], state[BLOCK:, :]
    return (2.0 * x - dot3(x, p)) / bound


def factor_kernel(
    total_tokens,
    tokens,
    out_grads,
    gradient,
    a_all,
    g_all,
    right,
    tok,
    grads,
    grad_in,
    a_part,
    a_core,
    a_ring,
    a_sum,
    a_second,
    a_line,
    a_third,
    a_cross,
    g_part,
    g_core,
    g_ring,
    g_sum,
    g_other,
    ns_in,
    full,
    state,
    load_sem,
    send_sem,
    recv_sem,
):
    dp, tensor = lax.axis_index("dp"), lax.axis_index("tensor")
    x, y_lo, c = dp // 4, (dp // 2) % 2, dp % 2
    y_hi, z = tensor // 4, tensor % 4
    y = y_hi * 2 + y_lo
    o = 1 - c

    def device(x_, y_, z_, c_):
        return {"dp": x_ * 4 + (y_ % 2) * 2 + c_, "tensor": (y_ // 2) * 4 + z_}

    def turn(position, by):
        return (position + by) % 4

    first, second = o * z + c * y, o * y + c * z

    def plane(first_, second_):
        return device(x, c * first_ + o * second_, o * first_ + c * second_, c)

    other_core = device(x, y, z, o)
    y_partner = y_hi * 2 + 1 - y_lo

    def a_core_of(y_, z_):
        return (y_ + z_ + 1) % 2

    on_a = c == a_core_of(y, z)
    on_g = jnp.logical_not(on_a)

    sent = []
    counters = {"send": 0, "recv": 0}

    def take(kind, count=1):
        at = counters[kind]
        counters[kind] += count
        return at

    def send(src, dst, recv_at, target, cond=None):
        send_at = take("send")

        def make():
            return pltpu.make_async_remote_copy(
                src_ref=src, dst_ref=dst, send_sem=send_sem.at[send_at], recv_sem=recv_sem.at[recv_at],
                device_id=target, device_id_type=MESH,
            )

        if cond is None:
            make().start()
        else:
            pl.when(cond)(lambda: make().start())
        sent.append((send_at, src.shape, cond))

    def await_recv(dst, recv_at):
        pltpu.make_async_remote_copy(
            src_ref=dst, dst_ref=dst, send_sem=send_sem.at[0], recv_sem=recv_sem.at[recv_at],
            device_id=other_core, device_id_type=MESH,
        ).wait_recv()

    def wait_sent(send_at, shape):
        like = {
            (ROWS, HALF): g_sum,
            (PIECE, HALF): a_line,
            (4, PIECE, HALF): a_sum,
            (CODED, HALF): a_all.at[0],
            (TOP, HALF): a_all.at[0, 0:TOP],
            (CODED - TOP, HALF): a_all.at[0, TOP:CODED],
        }[tuple(shape)]
        pltpu.make_async_remote_copy(
            src_ref=like, dst_ref=like, send_sem=send_sem.at[send_at], recv_sem=recv_sem.at[0],
            device_id=other_core, device_id_type=MESH,
        ).wait_send()

    def finish():
        for send_at, shape, cond in sent:
            if cond is None:
                wait_sent(send_at, shape)
            else:
                pl.when(cond)(functools.partial(wait_sent, send_at, shape))

    barrier = pltpu.get_barrier_semaphore()
    others = [other_core]
    for by in (1, 2, 3):
        others.append(device(turn(x, by), y, z, c))
        others.append(device(turn(x, by), y, z, o))
        others.append(device(x, turn(y, by), z, c))
        others.append(device(x, y, turn(z, by), c))
    for by in (1, 3):
        others.append(device(x, turn(y, by), z, o))
        others.append(device(x, y, turn(z, by), o))
    for target in others:
        pl.semaphore_signal(barrier, inc=1, device_id=target, device_id_type=MESH)

    token_load = pltpu.make_async_copy(tokens, tok, load_sem.at[8])
    token_load.start()
    gradient_load = pltpu.make_async_copy(gradient, grad_in, load_sem.at[9])

    def grad_load(at):
        i = at % 4
        core = o + (at // 4) * (c - o)
        block = 2 * turn(x, 1 + i) + (core + z) % 2
        return pltpu.make_async_copy(
            out_grads.at[:, pl.ds(pl.multiple_of(block * BLOCK, BLOCK), BLOCK)], grads.at[at], load_sem.at[at]
        )

    for at in range(8):
        grad_load(at).start()
    gradient_load.start()

    def grad_waits(stage):
        gradient_load.wait()
        for at in range(8):
            if stage == 1 or (stage <= 3 and at >= 4):
                grad_load(at).wait()

    token_load.wait()

    def a_gram(k, carry):
        v = tok[:, pl.ds(pl.multiple_of(k * BLOCK, BLOCK), BLOCK)]
        pack_into(a_part.at[0, k % 4, k // 4], a_part.at[1, k // 4, k % 4], gram(v))
        return carry

    lax.fori_loop(0, 16, a_gram, 0, unroll=4)
    pl.semaphore_wait(barrier, len(others))

    a_core_recv = take("recv", 4)
    for i in range(4):
        at = turn(first, 1 + i)
        send(a_part.at[o, :, at], a_core.at[:, at], a_core_recv + i, other_core)

    g_core_recv = take("recv", 4)
    g_core_send = take("send", 4)

    def to_core(i):
        return pltpu.make_async_remote_copy(
            src_ref=g_part.at[i], dst_ref=g_core.at[i], send_sem=send_sem.at[g_core_send + i],
            recv_sem=recv_sem.at[g_core_recv + i], device_id=other_core, device_id_type=MESH,
        )

    def g_gram(at):
        grad_load(at).wait()
        pack_into(g_part.at[at, 0:PIECE], g_part.at[at, PIECE:ROWS], gram(grads[at]))

    def their_gram(i, carry):
        g_gram(i)
        to_core(i).start()
        return carry

    def wait_to_core(i, carry):
        to_core(i).wait_send()
        return carry

    lax.fori_loop(0, 2, their_gram, 0, unroll=2)

    a_ring_recv = take("recv", 12)
    for i in range(4):
        at = turn(second, 1 + i)
        await_recv(a_core.at[:, at], a_core_recv + i)
        a_part[c, :, at] += a_core[:, at]
        for by in (1, 2, 3):
            send(
                a_part.at[c, turn(first, by), at], a_ring.at[3 - by, at], a_ring_recv + 3 * i + 3 - by,
                plane(turn(first, by), second),
            )

    lax.fori_loop(2, 4, their_gram, 0, unroll=2)

    g_ring_recv = take("recv", 3)
    g_ring_send = take("send", 3)

    def to_x(i):
        return pltpu.make_async_remote_copy(
            src_ref=g_part.at[4 + i], dst_ref=g_ring.at[2 - i], send_sem=send_sem.at[g_ring_send + i],
            recv_sem=recv_sem.at[g_ring_recv + 2 - i], device_id=device(turn(x, 1 + i), y, z, c), device_id_type=MESH,
        )

    def my_gram(i, carry):
        g_gram(4 + i)
        await_recv(g_core.at[i], g_core_recv + i)
        g_part[4 + i] += g_core[i]

        @pl.when(i < 3)
        def _():
            to_x(i).start()

        return carry

    def wait_to_x(i, carry):
        to_x(i).wait_send()
        return carry

    lax.fori_loop(0, 4, my_gram, 0, unroll=2)

    a_second_recv = take("recv", 3)
    for i in range(4):
        at = turn(second, 1 + i)
        for slot in range(3):
            await_recv(a_ring.at[slot, at], a_ring_recv + 3 * i + slot)
        a_sum[i] = (a_part[c, first, at] + a_ring[0, at]) + (a_ring[1, at] + a_ring[2, at])
        if i < 3:
            send(a_sum.at[i], a_second.at[2 - i], a_second_recv + 2 - i, plane(first, at))

    for slot in range(3):
        await_recv(g_ring.at[slot], g_ring_recv + slot)
    g_sum[...] = (g_part[7] + g_ring[0]) + (g_ring[1] + g_ring[2])
    g_y_recv = take("recv")
    send(g_sum, g_other, g_y_recv, device(x, y_partner, z, c), on_a)

    for slot in range(3):
        await_recv(a_second.at[slot], a_second_recv + slot)
    a_line[...] = (a_sum[3] + a_second[0]) + (a_second[1] + a_second[2])
    a_third_recv = take("recv", 6)
    a_cross_recv = take("recv")
    for by in (1, 2, 3):
        send(
            a_line, a_third.at[3 - by, c], a_third_recv + 2 * (3 - by) + c,
            device(turn(x, by), y, z, a_core_of(y, z)),
        )
    send(a_line, a_cross, a_cross_recv, other_core, on_g)

    @pl.when(on_g)
    def _():
        await_recv(g_other, g_y_recv)
        ns_in[...] = g_sum[...] + g_other[...]

    @pl.when(on_a)
    def _():
        await_recv(a_cross, a_cross_recv)
        for slot in range(3):
            for h in range(2):
                await_recv(a_third.at[slot, h], a_third_recv + 2 * slot + h)
        here = pl.ds(pl.multiple_of(c * PIECE, 8), PIECE)
        there = pl.ds(pl.multiple_of(o * PIECE, 8), PIECE)
        ns_in[here] = (a_line[...] + a_third[0, c]) + (a_third[1, c] + a_third[2, c])
        ns_in[there] = (a_cross[...] + a_third[0, o]) + (a_third[1, o] + a_third[2, o])

    g_mine = 2 * x + y_lo
    a_mine = 4 * y + z
    unpack_into(full, ns_in[...])
    full[...] = newton_inverse(full, state, total_tokens)

    g_x_recv = take("recv", 9)
    g_p_recv = take("recv", 2)
    g_copy_recv = take("recv", 8)
    g_sends = len(sent)

    @pl.when(on_g)
    def _():
        encode_into(g_all.at[g_mine], full[...])
        own = g_all.at[g_mine]
        halves = (pl.ds(0, TOP), pl.ds(TOP, CODED - TOP))
        for h, rows in enumerate(halves):
            send(own.at[rows], own.at[rows], g_p_recv + h, device(x, y_partner, z, o))
        for by in (1, 3, 2):
            send(own, own, g_x_recv + 3 - by, device(turn(x, by), y, z, c))
        send(own, own, g_copy_recv + g_mine, other_core)
        beside = 2 * x + 1 - y_lo
        held = g_all.at[beside]
        for h, rows in enumerate(halves):
            await_recv(held.at[rows], g_p_recv + h)
            for by in (1, 3, 2):
                send(held.at[rows], held.at[rows], g_x_recv + 3 + 3 * h + 3 - by, device(turn(x, by), y, z, c))
        send(held, held, g_copy_recv + beside, other_core)
        for slot in (0, 2, 1):
            block = 2 * turn(x, 1 + slot) + y_lo
            held = g_all.at[block]
            await_recv(held, g_x_recv + slot)
            send(held, held, g_copy_recv + block, other_core)
        for slot in (0, 2, 1):
            block = 2 * turn(x, 1 + slot) + 1 - y_lo
            held = g_all.at[block]
            for h, rows in enumerate(halves):
                await_recv(held.at[rows], g_x_recv + 3 + 3 * h + slot)
            send(held, held, g_copy_recv + block, other_core)

    g_sends = (g_sends, len(sent))

    a_y_recv = take("recv", 6)
    a_z_recv = take("recv", 6)
    a_top_recv = take("recv", 9)
    a_bottom_recv = take("recv", 9)
    a_copy_recv = take("recv", 16)
    a_sends = len(sent)

    def to_y(by):
        y_ = turn(y, by)
        return device(x, y_, z, a_core_of(y_, z))

    def to_z(by):
        z_ = turn(z, by)
        return device(x, y, z_, a_core_of(y, z_))

    @pl.when(on_a)
    def _():
        encode_into(a_all.at[a_mine], full[...])
        own = a_all.at[a_mine]
        own_top, own_bottom = a_all.at[a_mine, 0:TOP], a_all.at[a_mine, TOP:CODED]
        for by in (1, 3, 2):
            send(own_top, own_top, a_y_recv + 3 - by, to_y(by))
            send(own_bottom, own_bottom, a_z_recv + 3 - by, to_z(by))
        for by in (1, 3, 2):
            send(own_bottom, own_bottom, a_y_recv + 6 - by, to_y(by))
            send(own_top, own_top, a_z_recv + 6 - by, to_z(by))
        send(own, own, a_copy_recv + a_mine, other_core)
        for slot in (0, 2, 1):
            top = a_all.at[4 * turn(y, 1 + slot) + z, 0:TOP]
            await_recv(top, a_y_recv + slot)
            for by in (1, 3, 2):
                send(top, top, a_top_recv + 3 * slot + 3 - by, to_z(by))
            bottom = a_all.at[4 * y + turn(z, 1 + slot), TOP:CODED]
            await_recv(bottom, a_z_recv + slot)
            for by in (1, 3, 2):
                send(bottom, bottom, a_bottom_recv + 3 * slot + 3 - by, to_y(by))
        for slot in (0, 2, 1):
            block = 4 * turn(y, 1 + slot) + z
            await_recv(a_all.at[block, TOP:CODED], a_y_recv + 3 + slot)
            send(a_all.at[block], a_all.at[block], a_copy_recv + block, other_core)
            block = 4 * y + turn(z, 1 + slot)
            await_recv(a_all.at[block, 0:TOP], a_z_recv + 3 + slot)
            send(a_all.at[block], a_all.at[block], a_copy_recv + block, other_core)

    gradient_load.wait()

    def right_product(i, carry):
        j = 2 * turn(x, i % 4) + y_lo + (i // 4) * (1 - 2 * y_lo)

        @pl.when(on_a)
        def _():
            await_recv(g_all.at[j], g_copy_recv + j)

        columns = pl.ds(pl.multiple_of(j * BLOCK, BLOCK), BLOCK)
        decode_into(full, g_all[j])
        right[:, columns] = dot3(grad_in[:, columns], full[...])
        return carry

    lax.fori_loop(0, 8, right_product, 0, unroll=2)

    @pl.when(on_a)
    def _():
        for slot_y in (0, 2, 1):
            for slot_z in (0, 2, 1):
                block = 4 * turn(y, 1 + slot_y) + turn(z, 1 + slot_z)
                await_recv(a_all.at[block, 0:TOP], a_top_recv + 3 * slot_y + slot_z)
                await_recv(a_all.at[block, TOP:CODED], a_bottom_recv + 3 * slot_z + slot_y)
                send(a_all.at[block], a_all.at[block], a_copy_recv + block, other_core)

    a_sends = (a_sends, len(sent))

    @pl.when(on_g)
    def _():
        def copied(block, carry):
            await_recv(a_all.at[block], a_copy_recv + block)
            return carry

        lax.fori_loop(0, 16, copied, 0)

    for (start, stop), held_here in ((g_sends, on_g), (a_sends, on_a)):
        for index in range(start, stop):
            sent[index] = (*sent[index][:2], held_here)
    lax.fori_loop(0, 4, wait_to_core, 0)
    lax.fori_loop(0, 3, wait_to_x, 0)
    finish()


def factors(tokens, out_grads, gradient, total_tokens):
    vmem = pl.BlockSpec(memory_space=pltpu.VMEM)
    anywhere = pl.BlockSpec(memory_space=pltpu.HBM)

    def pieces(*lead):
        return pltpu.VMEM((*lead, PIECE, HALF), F32)

    def blocks(*lead):
        return pltpu.VMEM((*lead, ROWS, HALF), F32)

    tokens, out_grads, gradient = (
        pltpu.with_memory_space_constraint(v, pltpu.HBM) for v in (tokens, out_grads, gradient)
    )
    return pl.pallas_call(
        functools.partial(factor_kernel, total_tokens),
        out_shape=(
            jax.ShapeDtypeStruct((16, CODED, HALF), jnp.int32),
            jax.ShapeDtypeStruct((8, CODED, HALF), jnp.int32),
            jax.ShapeDtypeStruct(gradient.shape, F32),
        ),
        in_specs=[anywhere, anywhere, anywhere],
        out_specs=(vmem, vmem, vmem),
        scratch_shapes=[
            pltpu.VMEM(tokens.shape, BF16),
            pltpu.VMEM((8, 2048, BLOCK), BF16),
            pltpu.VMEM(gradient.shape, F32),
            pieces(2, 4, 4),
            pieces(4, 4),
            pieces(3, 4),
            pieces(4),
            pieces(3),
            pieces(),
            pieces(3, 2),
            pieces(),
            blocks(8),
            blocks(4),
            blocks(3),
            blocks(),
            blocks(),
            blocks(),
            pltpu.VMEM((BLOCK, BLOCK), F32),
            pltpu.VMEM((2 * BLOCK, BLOCK), F32),
            pltpu.SemaphoreType.DMA((10,)),
            pltpu.SemaphoreType.DMA((128,)),
            pltpu.SemaphoreType.DMA((128,)),
        ],
        compiler_params=pltpu.CompilerParams(
            collective_id=0, has_side_effects=True, vmem_limit_bytes=32 * 2**20
        ),
        name="factors",
    )(tokens, out_grads, gradient)


def apply_kernel(owners, a_all, g_all, right, out, inverses, left, result, placed, out_sem):
    dp = lax.axis_index("dp")
    width = right.shape[1] // 4
    decode_into(left, a_all[dp])

    def out_copy(q):
        columns = pl.ds(pl.multiple_of(q * width, width), width)
        return pltpu.make_async_copy(result.at[:, columns], out.at[:, columns], out_sem.at[q])

    def left_product(q, carry):
        columns = pl.ds(pl.multiple_of(q * width, width), width)
        result[:, columns] = dot3(left[...], right[:, columns])
        out_copy(q).start()
        return carry

    lax.fori_loop(0, 4, left_product, 0, unroll=4)

    def scan(b, carry):
        seen, slots = carry
        hit = owners[0, b] == dp
        slots = tuple(jnp.where(jnp.logical_and(hit, seen == s), b, slot) for s, slot in enumerate(slots))
        return seen + hit.astype(jnp.int32), slots

    _, slots = lax.fori_loop(0, 24, scan, (jnp.int32(0), (jnp.int32(-1),) * 3))
    for s, chosen in enumerate(slots):
        @pl.when(chosen < 0)
        def _():
            placed[s] = jnp.zeros((BLOCK, BLOCK), F32)

        @pl.when(jnp.logical_and(chosen >= 0, chosen < 16))
        def _():
            decode_into(placed.at[s], a_all[chosen])

        @pl.when(chosen >= 16)
        def _():
            decode_into(placed.at[s], g_all[chosen - 16])

        pltpu.make_async_copy(placed.at[s], inverses.at[0, 0, s], out_sem.at[4 + s]).start()
    for q in range(4):
        out_copy(q).wait()
    for s in range(3):
        pltpu.make_async_copy(placed.at[s], inverses.at[0, 0, s], out_sem.at[4 + s]).wait()


def apply(owners, a_all, g_all, right):
    vmem = pl.BlockSpec(memory_space=pltpu.VMEM)
    anywhere = pl.BlockSpec(memory_space=pl.ANY)
    return pl.pallas_call(
        apply_kernel,
        out_shape=(
            jax.ShapeDtypeStruct(right.shape, F32),
            jax.ShapeDtypeStruct((1, 1, 3, BLOCK, BLOCK), F32),
        ),
        in_specs=[pl.BlockSpec(memory_space=pltpu.SMEM), vmem, vmem, vmem],
        out_specs=(anywhere, anywhere),
        scratch_shapes=[
            pltpu.VMEM((BLOCK, BLOCK), F32),
            pltpu.VMEM(right.shape, F32),
            pltpu.VMEM((3, BLOCK, BLOCK), F32),
            pltpu.SemaphoreType.DMA((7,)),
        ],
        compiler_params=pltpu.CompilerParams(vmem_limit_bytes=32 * 2**20),
        name="apply",
    )(owners, a_all, g_all, right)


def on_device(tokens, out_grads, gradient, owners):
    total_tokens = tokens.shape[0] * lax.axis_size("tensor") * lax.axis_size("dp")
    a_all, g_all, right = factors(tokens, out_grads, gradient, total_tokens)
    return apply(owners, a_all, g_all, right)


def solution(mesh):
    placed = (P(("dp", "tensor"), None), P("dp", "tensor"), P("dp", "tensor"), P("tensor", None))
    return jax.shard_map(
        on_device,
        mesh=mesh,
        in_specs=placed,
        out_specs=(P("dp", "tensor"), P("tensor", "dp", None, None, None)),
        check_vma=False,
    )
```

```python
import functools
import jax
import jax.numpy as jnp
from jax import lax
from jax.experimental import pallas as pl
from jax.experimental.pallas import tpu as pltpu
from jax.sharding import PartitionSpec as P

BLOCK = 256
HALF = 128
PIECE = 136
ROWS = 2 * PIECE
GROUP = 32
TOP = 3 * GROUP + 8
CODED = TOP + 3 * GROUP
NS_ITERS = 12
COARSE = 4
DAMPING = 0.01
MESH = pl.DeviceIdType.MESH
F32 = jnp.float32
BF16 = jnp.bfloat16


def iotas(n):
    return (
        lax.broadcasted_iota(jnp.int32, (n, n), 0),
        lax.broadcasted_iota(jnp.int32, (n, n), 1),
    )


def pack_into(top, bottom, full):
    row, col = iotas(HALF)
    upper_left, lower_right = full[:HALF, :HALF], full[HALF:, HALF:]
    top[0:HALF, :] = jnp.where(row >= col, upper_left, lower_right)
    diagonal = jnp.sum(jnp.where(row == col, lower_right, 0.0), axis=0, keepdims=True)
    top[HALF:PIECE, :] = jnp.broadcast_to(diagonal, (PIECE - HALF, HALF))
    bottom[0:HALF, :] = full[HALF:, :HALF]
    bottom[HALF:PIECE, :] = jnp.zeros((PIECE - HALF, HALF), F32)


def unpack_into(dst, packed):
    row, col = iotas(HALF)
    both, below = packed[0:HALF, :], packed[PIECE:PIECE + HALF, :]
    diagonal = packed[HALF:HALF + 1, :]
    turned = both.T
    dst[0:HALF, 0:HALF] = jnp.where(row >= col, both, turned)
    dst[HALF:BLOCK, HALF:BLOCK] = jnp.where(row < col, both, jnp.where(row == col, diagonal, turned))
    dst[HALF:BLOCK, 0:HALF] = below
    dst[0:HALF, HALF:BLOCK] = below.T


def to_words(v):
    first, second, third, fourth = (v[k * GROUP:(k + 1) * GROUP] for k in range(4))
    return (
        (first & 0xFFFFFF) | (fourth << 24),
        (second & 0xFFFFFF) | ((fourth >> 8) << 24),
        (third & 0xFFFFFF) | ((fourth >> 16) << 24),
    )


def from_words(words):
    parts = [words[k * GROUP:(k + 1) * GROUP] for k in range(3)]
    low, mid, high = parts
    fourth = ((low >> 24) & 0xFF) | (((mid >> 24) & 0xFF) << 8) | ((high >> 24) << 16)
    return jnp.concatenate([(w << 8) >> 8 for w in parts] + [fourth], axis=0)


def encode_into(dst, full):
    row, col = iotas(HALF)
    peak = jnp.max(jnp.max(jnp.abs(full), axis=0, keepdims=True), axis=1, keepdims=True)
    exponent = jnp.floor(jnp.log2(peak) + 1.01)
    scaled = full * (8388608.0 / jnp.exp2(exponent))
    whole = (scaled + jnp.where(scaled >= 0.0, 0.5, -0.5)).astype(jnp.int32)
    upper_left, lower_right = whole[:HALF, :HALF], whole[HALF:, HALF:]
    for k, words in enumerate(to_words(jnp.where(row >= col, upper_left, lower_right))):
        dst[k * GROUP:(k + 1) * GROUP, :] = words
    diagonal = jnp.sum(jnp.where(row == col, lower_right, 0), axis=0, keepdims=True)
    tile_row = lax.broadcasted_iota(jnp.int32, (8, HALF), 0)
    dst[3 * GROUP:TOP, :] = jnp.where(tile_row == 0, diagonal, exponent.astype(jnp.int32))
    for k, words in enumerate(to_words(whole[HALF:, :HALF])):
        dst[TOP + k * GROUP:TOP + (k + 1) * GROUP, :] = words


def decode_into(dst, coded):
    row, col = iotas(HALF)
    scale = jnp.exp2(coded[3 * GROUP + 1:3 * GROUP + 2, :].astype(F32)) * (1.0 / 8388608.0)
    both = from_words(coded[:3 * GROUP]).astype(F32) * scale
    diagonal = coded[3 * GROUP:3 * GROUP + 1, :].astype(F32) * scale
    below = from_words(coded[TOP:]).astype(F32) * scale
    turned = both.T
    dst[0:HALF, 0:HALF] = jnp.where(row >= col, both, turned)
    dst[HALF:BLOCK, HALF:BLOCK] = jnp.where(row < col, both, jnp.where(row == col, diagonal, turned))
    dst[HALF:BLOCK, 0:HALF] = below
    dst[0:HALF, HALF:BLOCK] = below.T


def bdot(a, b):
    return jnp.dot(a, b, preferred_element_type=F32)


def gram(v):
    return lax.dot_general(v, v, (((0,), (0,)), ((), ())), preferred_element_type=F32)


def split2(v):
    high = v.astype(BF16)
    return high, (v - high.astype(F32)).astype(BF16)


def split3(v):
    high = v.astype(BF16)
    rest = v - high.astype(F32)
    mid = rest.astype(BF16)
    return high, mid, (rest - mid.astype(F32)).astype(BF16)


def dot3(a, b):
    ah, al = split2(a)
    bh, bl = split2(b)
    return (bdot(ah, bl) + bdot(al, bh)) + bdot(ah, bh)


def newton_inverse(full, state, total_tokens):
    row, col = iotas(BLOCK)
    on_diagonal = row == col
    cov = full[...] * (1.0 / total_tokens)
    trace = jnp.sum(jnp.where(on_diagonal, cov, 0.0))
    damped = cov + jnp.where(on_diagonal, DAMPING / BLOCK * trace, 0.0)
    bound = jnp.max(jnp.sum(jnp.abs(damped), axis=0, keepdims=True), axis=1, keepdims=True)
    p = damped / bound
    state[BLOCK:, :] = jnp.where(on_diagonal, 2.0, 0.0) - p
    state[:BLOCK, :] = 2.0 * p - jnp.dot(p, p, precision=lax.Precision.HIGHEST)

    def sweep(fine, index, carry):
        p, x = state[:BLOCK, :], state[BLOCK:, :]
        ph, pm, pl_ = split3(p)
        xh, xm = split2(x)
        cross = bdot(pm, ph) + bdot(ph, pm)
        if fine:
            cross = (bdot(ph, pl_) + bdot(pl_, ph) + bdot(pm, pm)) + cross
        state[:BLOCK, :] = 2.0 * p - (cross + bdot(ph, ph))
        state[BLOCK:, :] = 2.0 * x - ((bdot(xm, ph) + bdot(xh, pm)) + bdot(xh, ph))
        return carry

    lax.fori_loop(0, NS_ITERS - 2 - COARSE, functools.partial(sweep, True), 0)
    lax.fori_loop(0, COARSE, functools.partial(sweep, False), 0)
    p, x = state[:BLOCK, :], state[BLOCK:, :]
    return (2.0 * x - dot3(x, p)) / bound


def factor_kernel(
    total_tokens,
    tokens,
    out_grads,
    gradient,
    a_all,
    g_all,
    right,
    tok,
    grads,
    grad_in,
    a_part,
    a_core,
    a_ring,
    a_sum,
    a_second,
    a_line,
    a_third,
    a_cross,
    g_part,
    g_core,
    g_ring,
    g_sum,
    g_other,
    ns_in,
    full,
    state,
    load_sem,
    send_sem,
    recv_sem,
):
    dp, tensor = lax.axis_index("dp"), lax.axis_index("tensor")
    x, y_lo, c = dp // 4, (dp // 2) % 2, dp % 2
    y_hi, z = tensor // 4, tensor % 4
    y = y_hi * 2 + y_lo
    o = 1 - c

    def device(x_, y_, z_, c_):
        return {"dp": x_ * 4 + (y_ % 2) * 2 + c_, "tensor": (y_ // 2) * 4 + z_}

    def turn(position, by):
        return (position + by) % 4

    first, second = o * z + c * y, o * y + c * z

    def plane(first_, second_):
        return device(x, c * first_ + o * second_, o * first_ + c * second_, c)

    other_core = device(x, y, z, o)
    y_partner = y_hi * 2 + 1 - y_lo

    def a_core_of(y_, z_):
        return (y_ + z_ + 1) % 2

    on_a = c == a_core_of(y, z)
    on_g = jnp.logical_not(on_a)

    sent = []
    counters = {"send": 0, "recv": 0}

    def take(kind, count=1):
        at = counters[kind]
        counters[kind] += count
        return at

    def send(src, dst, recv_at, target, cond=None):
        send_at = take("send")

        def make():
            return pltpu.make_async_remote_copy(
                src_ref=src, dst_ref=dst, send_sem=send_sem.at[send_at], recv_sem=recv_sem.at[recv_at],
                device_id=target, device_id_type=MESH,
            )

        if cond is None:
            make().start()
        else:
            pl.when(cond)(lambda: make().start())
        sent.append((send_at, src.shape, cond))

    def await_recv(dst, recv_at):
        pltpu.make_async_remote_copy(
            src_ref=dst, dst_ref=dst, send_sem=send_sem.at[0], recv_sem=recv_sem.at[recv_at],
            device_id=other_core, device_id_type=MESH,
        ).wait_recv()

    def wait_sent(send_at, shape):
        like = {
            (ROWS, HALF): g_sum,
            (PIECE, HALF): a_line,
            (4, PIECE, HALF): a_sum,
            (CODED, HALF): a_all.at[0],
            (TOP, HALF): a_all.at[0, 0:TOP],
            (CODED - TOP, HALF): a_all.at[0, TOP:CODED],
        }[tuple(shape)]
        pltpu.make_async_remote_copy(
            src_ref=like, dst_ref=like, send_sem=send_sem.at[send_at], recv_sem=recv_sem.at[0],
            device_id=other_core, device_id_type=MESH,
        ).wait_send()

    def finish():
        for send_at, shape, cond in sent:
            if cond is None:
                wait_sent(send_at, shape)
            else:
                pl.when(cond)(functools.partial(wait_sent, send_at, shape))

    barrier = pltpu.get_barrier_semaphore()
    others = []
    for by in (2, 1, 3):
        others.append(device(turn(x, by), y, z, c))
        others.append(device(turn(x, by), y, z, o))
        others.append(device(x, turn(y, by), z, c))
        others.append(device(x, y, turn(z, by), c))
    for by in (1, 3):
        others.append(device(x, turn(y, by), z, o))
        others.append(device(x, y, turn(z, by), o))
    others.append(other_core)
    for target in others:
        pl.semaphore_signal(barrier, inc=1, device_id=target, device_id_type=MESH)

    token_load = pltpu.make_async_copy(tokens, tok, load_sem.at[8])
    token_load.start()
    gradient_load = pltpu.make_async_copy(gradient, grad_in, load_sem.at[9])

    def grad_load(at):
        by = (2, 1, 3, 0)[at % 4]
        core = o + (at // 4) * (c - o)
        block = 2 * turn(x, by) + (core + z) % 2
        return pltpu.make_async_copy(
            out_grads.at[:, pl.ds(pl.multiple_of(block * BLOCK, BLOCK), BLOCK)], grads.at[at], load_sem.at[at]
        )


    def grad_waits(stage):
        gradient_load.wait()
        for at in range(8):
            if stage == 1 or (stage <= 3 and at >= 4):
                grad_load(at).wait()

    token_load.wait()
    for at in range(8):
        grad_load(at).start()
    gradient_load.start()

    def a_gram(k, carry):
        v = tok[:, pl.ds(pl.multiple_of(k * BLOCK, BLOCK), BLOCK)]
        pack_into(a_part.at[0, k % 4, k // 4], a_part.at[1, k // 4, k % 4], gram(v))
        return carry

    lax.fori_loop(0, 16, a_gram, 0, unroll=4)
    pl.semaphore_wait(barrier, len(others))

    a_core_recv = take("recv", 4)
    orders = (2, 1, 3, 0)
    for i in range(4):
        at = turn(first, orders[i])
        send(a_part.at[o, :, at], a_core.at[:, at], a_core_recv + i, other_core)

    g_core_recv = take("recv", 4)

    def g_gram(at):
        grad_load(at).wait()
        pack_into(g_part.at[at, 0:PIECE], g_part.at[at, PIECE:ROWS], gram(grads[at]))

    def their_gram(i):
        g_gram(i)
        send(g_part.at[i], g_core.at[i], g_core_recv + i, other_core)

    their_gram(0)
    their_gram(1)

    a_ring_recv = take("recv", 12)
    for i in range(4):
        at = turn(second, orders[i])
        await_recv(a_core.at[:, at], a_core_recv + i)
        a_part[c, :, at] += a_core[:, at]
        for by in (2, 1, 3):
            send(
                a_part.at[c, turn(first, by), at], a_ring.at[3 - by, at], a_ring_recv + 3 * i + 3 - by,
                plane(turn(first, by), second),
            )

    their_gram(2)
    their_gram(3)

    g_ring_recv = take("recv", 3)
    for i in range(4):
        g_gram(4 + i)
        await_recv(g_core.at[i], g_core_recv + i)
        g_part[4 + i] += g_core[i]
        if i < 3:
            slot = 3 - orders[i]
            send(g_part.at[4 + i], g_ring.at[slot], g_ring_recv + slot, device(turn(x, orders[i]), y, z, c))

    a_second_recv = take("recv", 3)
    for i in range(4):
        at = turn(second, orders[i])
        for slot in range(3):
            await_recv(a_ring.at[slot, at], a_ring_recv + 3 * i + slot)
        a_sum[i] = (a_part[c, first, at] + a_ring[0, at]) + (a_ring[1, at] + a_ring[2, at])
        if i < 3:
            slot = 3 - orders[i]
            send(a_sum.at[i], a_second.at[slot], a_second_recv + slot, plane(first, at))

    for slot in range(3):
        await_recv(g_ring.at[slot], g_ring_recv + slot)
    g_sum[...] = (g_part[7] + g_ring[0]) + (g_ring[1] + g_ring[2])
    g_y_recv = take("recv")
    send(g_sum, g_other, g_y_recv, device(x, y_partner, z, c), on_a)

    for slot in range(3):
        await_recv(a_second.at[slot], a_second_recv + slot)
    a_line[...] = (a_sum[3] + a_second[0]) + (a_second[1] + a_second[2])
    a_third_recv = take("recv", 6)
    a_cross_recv = take("recv")
    for by in (2, 1, 3):
        send(
            a_line, a_third.at[3 - by, c], a_third_recv + 2 * (3 - by) + c,
            device(turn(x, by), y, z, a_core_of(y, z)),
        )
    send(a_line, a_cross, a_cross_recv, other_core, on_g)

    @pl.when(on_g)
    def _():
        await_recv(g_other, g_y_recv)
        ns_in[...] = g_sum[...] + g_other[...]

    @pl.when(on_a)
    def _():
        await_recv(a_cross, a_cross_recv)
        for slot in range(3):
            for h in range(2):
                await_recv(a_third.at[slot, h], a_third_recv + 2 * slot + h)
        here = pl.ds(pl.multiple_of(c * PIECE, 8), PIECE)
        there = pl.ds(pl.multiple_of(o * PIECE, 8), PIECE)
        ns_in[here] = (a_line[...] + a_third[0, c]) + (a_third[1, c] + a_third[2, c])
        ns_in[there] = (a_cross[...] + a_third[0, o]) + (a_third[1, o] + a_third[2, o])

    g_mine = 2 * x + y_lo
    a_mine = 4 * y + z
    unpack_into(full, ns_in[...])
    full[...] = newton_inverse(full, state, total_tokens)

    g_x_recv = take("recv", 9)
    g_p_recv = take("recv", 2)
    g_copy_recv = take("recv", 8)
    g_sends = len(sent)

    @pl.when(on_g)
    def _():
        encode_into(g_all.at[g_mine], full[...])
        own = g_all.at[g_mine]
        halves = (pl.ds(0, TOP), pl.ds(TOP, CODED - TOP))
        for h, rows in enumerate(halves):
            send(own.at[rows], own.at[rows], g_p_recv + h, device(x, y_partner, z, o))
        for by in (1, 3, 2):
            send(own, own, g_x_recv + 3 - by, device(turn(x, by), y, z, c))
        send(own, own, g_copy_recv + g_mine, other_core)
        beside = 2 * x + 1 - y_lo
        held = g_all.at[beside]
        for h, rows in enumerate(halves):
            await_recv(held.at[rows], g_p_recv + h)
            for by in (1, 3, 2):
                send(held.at[rows], held.at[rows], g_x_recv + 3 + 3 * h + 3 - by, device(turn(x, by), y, z, c))
        send(held, held, g_copy_recv + beside, other_core)
        for slot in (0, 2, 1):
            block = 2 * turn(x, 1 + slot) + y_lo
            held = g_all.at[block]
            await_recv(held, g_x_recv + slot)
            send(held, held, g_copy_recv + block, other_core)
        for slot in (0, 2, 1):
            block = 2 * turn(x, 1 + slot) + 1 - y_lo
            held = g_all.at[block]
            for h, rows in enumerate(halves):
                await_recv(held.at[rows], g_x_recv + 3 + 3 * h + slot)
            send(held, held, g_copy_recv + block, other_core)

    g_sends = (g_sends, len(sent))

    a_y_recv = take("recv", 6)
    a_z_recv = take("recv", 6)
    a_top_recv = take("recv", 9)
    a_bottom_recv = take("recv", 9)
    a_copy_recv = take("recv", 16)
    a_sends = len(sent)

    def to_y(by):
        y_ = turn(y, by)
        return device(x, y_, z, a_core_of(y_, z))

    def to_z(by):
        z_ = turn(z, by)
        return device(x, y, z_, a_core_of(y, z_))

    @pl.when(on_a)
    def _():
        encode_into(a_all.at[a_mine], full[...])
        own = a_all.at[a_mine]
        own_top, own_bottom = a_all.at[a_mine, 0:TOP], a_all.at[a_mine, TOP:CODED]
        for by in (1, 3, 2):
            send(own_top, own_top, a_y_recv + 3 - by, to_y(by))
            send(own_bottom, own_bottom, a_z_recv + 3 - by, to_z(by))
        for by in (1, 3, 2):
            send(own_bottom, own_bottom, a_y_recv + 6 - by, to_y(by))
            send(own_top, own_top, a_z_recv + 6 - by, to_z(by))
        send(own, own, a_copy_recv + a_mine, other_core)
        for slot in (0, 2, 1):
            top = a_all.at[4 * turn(y, 1 + slot) + z, 0:TOP]
            await_recv(top, a_y_recv + slot)
            for by in (1, 3, 2):
                send(top, top, a_top_recv + 3 * slot + 3 - by, to_z(by))
            bottom = a_all.at[4 * y + turn(z, 1 + slot), TOP:CODED]
            await_recv(bottom, a_z_recv + slot)
            for by in (1, 3, 2):
                send(bottom, bottom, a_bottom_recv + 3 * slot + 3 - by, to_y(by))
        for slot in (0, 2, 1):
            block = 4 * turn(y, 1 + slot) + z
            await_recv(a_all.at[block, TOP:CODED], a_y_recv + 3 + slot)
            send(a_all.at[block], a_all.at[block], a_copy_recv + block, other_core)
            block = 4 * y + turn(z, 1 + slot)
            await_recv(a_all.at[block, 0:TOP], a_z_recv + 3 + slot)
            send(a_all.at[block], a_all.at[block], a_copy_recv + block, other_core)

    gradient_load.wait()

    def right_product(i, carry):
        j = 2 * turn(x, i % 4) + y_lo + (i // 4) * (1 - 2 * y_lo)

        @pl.when(on_a)
        def _():
            await_recv(g_all.at[j], g_copy_recv + j)

        columns = pl.ds(pl.multiple_of(j * BLOCK, BLOCK), BLOCK)
        decode_into(full, g_all[j])
        right[:, columns] = dot3(grad_in[:, columns], full[...])
        return carry

    lax.fori_loop(0, 8, right_product, 0, unroll=2)

    @pl.when(on_a)
    def _():
        for slot_y in (0, 2, 1):
            for slot_z in (0, 2, 1):
                block = 4 * turn(y, 1 + slot_y) + turn(z, 1 + slot_z)
                await_recv(a_all.at[block, 0:TOP], a_top_recv + 3 * slot_y + slot_z)
                await_recv(a_all.at[block, TOP:CODED], a_bottom_recv + 3 * slot_z + slot_y)
                send(a_all.at[block], a_all.at[block], a_copy_recv + block, other_core)

    a_sends = (a_sends, len(sent))

    @pl.when(on_g)
    def _():
        def copied(block, carry):
            await_recv(a_all.at[block], a_copy_recv + block)
            return carry

        lax.fori_loop(0, 16, copied, 0)

    for (start, stop), held_here in ((g_sends, on_g), (a_sends, on_a)):
        for index in range(start, stop):
            sent[index] = (*sent[index][:2], held_here)
    finish()


def factors(tokens, out_grads, gradient, total_tokens):
    vmem = pl.BlockSpec(memory_space=pltpu.VMEM)
    anywhere = pl.BlockSpec(memory_space=pltpu.HBM)

    def pieces(*lead):
        return pltpu.VMEM((*lead, PIECE, HALF), F32)

    def blocks(*lead):
        return pltpu.VMEM((*lead, ROWS, HALF), F32)

    tokens, out_grads, gradient = (
        pltpu.with_memory_space_constraint(v, pltpu.HBM) for v in (tokens, out_grads, gradient)
    )
    return pl.pallas_call(
        functools.partial(factor_kernel, total_tokens),
        out_shape=(
            jax.ShapeDtypeStruct((16, CODED, HALF), jnp.int32),
            jax.ShapeDtypeStruct((8, CODED, HALF), jnp.int32),
            jax.ShapeDtypeStruct(gradient.shape, F32),
        ),
        in_specs=[anywhere, anywhere, anywhere],
        out_specs=(vmem, vmem, vmem),
        scratch_shapes=[
            pltpu.VMEM(tokens.shape, BF16),
            pltpu.VMEM((8, 2048, BLOCK), BF16),
            pltpu.VMEM(gradient.shape, F32),
            pieces(2, 4, 4),
            pieces(4, 4),
            pieces(3, 4),
            pieces(4),
            pieces(3),
            pieces(),
            pieces(3, 2),
            pieces(),
            blocks(8),
            blocks(4),
            blocks(3),
            blocks(),
            blocks(),
            blocks(),
            pltpu.VMEM((BLOCK, BLOCK), F32),
            pltpu.VMEM((2 * BLOCK, BLOCK), F32),
            pltpu.SemaphoreType.DMA((10,)),
            pltpu.SemaphoreType.DMA((128,)),
            pltpu.SemaphoreType.DMA((128,)),
        ],
        compiler_params=pltpu.CompilerParams(
            collective_id=0, has_side_effects=True, vmem_limit_bytes=32 * 2**20
        ),
        name="factors",
    )(tokens, out_grads, gradient)


def apply_kernel(owners, a_all, g_all, right, out, inverses, left, result, placed, out_sem):
    dp = lax.axis_index("dp")
    width = right.shape[1] // 4
    decode_into(left, a_all[dp])

    def out_copy(q):
        columns = pl.ds(pl.multiple_of(q * width, width), width)
        return pltpu.make_async_copy(result.at[:, columns], out.at[:, columns], out_sem.at[q])

    def left_product(q, carry):
        columns = pl.ds(pl.multiple_of(q * width, width), width)
        result[:, columns] = dot3(left[...], right[:, columns])
        out_copy(q).start()
        return carry

    lax.fori_loop(0, 4, left_product, 0, unroll=4)

    def scan(b, carry):
        seen, slots = carry
        hit = owners[0, b] == dp
        slots = tuple(jnp.where(jnp.logical_and(hit, seen == s), b, slot) for s, slot in enumerate(slots))
        return seen + hit.astype(jnp.int32), slots

    _, slots = lax.fori_loop(0, 24, scan, (jnp.int32(0), (jnp.int32(-1),) * 3))
    for s, chosen in enumerate(slots):
        @pl.when(chosen < 0)
        def _():
            placed[s] = jnp.zeros((BLOCK, BLOCK), F32)

        @pl.when(jnp.logical_and(chosen >= 0, chosen < 16))
        def _():
            decode_into(placed.at[s], a_all[chosen])

        @pl.when(chosen >= 16)
        def _():
            decode_into(placed.at[s], g_all[chosen - 16])

        pltpu.make_async_copy(placed.at[s], inverses.at[0, 0, s], out_sem.at[4 + s]).start()
    for q in range(4):
        out_copy(q).wait()
    for s in range(3):
        pltpu.make_async_copy(placed.at[s], inverses.at[0, 0, s], out_sem.at[4 + s]).wait()


def apply(owners, a_all, g_all, right):
    vmem = pl.BlockSpec(memory_space=pltpu.VMEM)
    anywhere = pl.BlockSpec(memory_space=pl.ANY)
    return pl.pallas_call(
        apply_kernel,
        out_shape=(
            jax.ShapeDtypeStruct(right.shape, F32),
            jax.ShapeDtypeStruct((1, 1, 3, BLOCK, BLOCK), F32),
        ),
        in_specs=[pl.BlockSpec(memory_space=pltpu.SMEM), vmem, vmem, vmem],
        out_specs=(anywhere, anywhere),
        scratch_shapes=[
            pltpu.VMEM((BLOCK, BLOCK), F32),
            pltpu.VMEM(right.shape, F32),
            pltpu.VMEM((3, BLOCK, BLOCK), F32),
            pltpu.SemaphoreType.DMA((7,)),
        ],
        compiler_params=pltpu.CompilerParams(vmem_limit_bytes=32 * 2**20),
        name="apply",
    )(owners, a_all, g_all, right)


def on_device(tokens, out_grads, gradient, owners):
    total_tokens = tokens.shape[0] * lax.axis_size("tensor") * lax.axis_size("dp")
    a_all, g_all, right = factors(tokens, out_grads, gradient, total_tokens)
    return apply(owners, a_all, g_all, right)


def solution(mesh):
    placed = (P(("dp", "tensor"), None), P("dp", "tensor"), P("dp", "tensor"), P("tensor", None))
    return jax.shard_map(
        on_device,
        mesh=mesh,
        in_specs=placed,
        out_specs=(P("dp", "tensor"), P("tensor", "dp", None, None, None)),
        check_vma=False,
    )
```

```python
import functools
import jax
import jax.numpy as jnp
from jax import lax
from jax.experimental import pallas as pl
from jax.experimental.pallas import tpu as pltpu
from jax.sharding import PartitionSpec as P

BLOCK = 256
HALF = 128
PIECE = 136
ROWS = 2 * PIECE
GROUP = 32
TOP = 3 * GROUP + 8
CODED = TOP + 3 * GROUP
NS_ITERS = 12
COARSE = 4
DAMPING = 0.01
MESH = pl.DeviceIdType.MESH
F32 = jnp.float32
BF16 = jnp.bfloat16


def iotas(n):
    return (
        lax.broadcasted_iota(jnp.int32, (n, n), 0),
        lax.broadcasted_iota(jnp.int32, (n, n), 1),
    )


def pack_into(top, bottom, full):
    row, col = iotas(HALF)
    upper_left, lower_right = full[:HALF, :HALF], full[HALF:, HALF:]
    top[0:HALF, :] = jnp.where(row >= col, upper_left, lower_right)
    diagonal = jnp.sum(jnp.where(row == col, lower_right, 0.0), axis=0, keepdims=True)
    top[HALF:PIECE, :] = jnp.broadcast_to(diagonal, (PIECE - HALF, HALF))
    bottom[0:HALF, :] = full[HALF:, :HALF]
    bottom[HALF:PIECE, :] = jnp.zeros((PIECE - HALF, HALF), F32)


def unpack_into(dst, packed):
    row, col = iotas(HALF)
    both, below = packed[0:HALF, :], packed[PIECE:PIECE + HALF, :]
    diagonal = packed[HALF:HALF + 1, :]
    turned = both.T
    dst[0:HALF, 0:HALF] = jnp.where(row >= col, both, turned)
    dst[HALF:BLOCK, HALF:BLOCK] = jnp.where(row < col, both, jnp.where(row == col, diagonal, turned))
    dst[HALF:BLOCK, 0:HALF] = below
    dst[0:HALF, HALF:BLOCK] = below.T


def to_words(v):
    first, second, third, fourth = (v[k * GROUP:(k + 1) * GROUP] for k in range(4))
    return (
        (first & 0xFFFFFF) | (fourth << 24),
        (second & 0xFFFFFF) | ((fourth >> 8) << 24),
        (third & 0xFFFFFF) | ((fourth >> 16) << 24),
    )


def from_words(words):
    parts = [words[k * GROUP:(k + 1) * GROUP] for k in range(3)]
    low, mid, high = parts
    fourth = ((low >> 24) & 0xFF) | (((mid >> 24) & 0xFF) << 8) | ((high >> 24) << 16)
    return jnp.concatenate([(w << 8) >> 8 for w in parts] + [fourth], axis=0)


def encode_into(dst, full):
    row, col = iotas(HALF)
    peak = jnp.max(jnp.max(jnp.abs(full), axis=0, keepdims=True), axis=1, keepdims=True)
    exponent = jnp.floor(jnp.log2(peak) + 1.01)
    scaled = full * (8388608.0 / jnp.exp2(exponent))
    whole = (scaled + jnp.where(scaled >= 0.0, 0.5, -0.5)).astype(jnp.int32)
    upper_left, lower_right = whole[:HALF, :HALF], whole[HALF:, HALF:]
    for k, words in enumerate(to_words(jnp.where(row >= col, upper_left, lower_right))):
        dst[k * GROUP:(k + 1) * GROUP, :] = words
    diagonal = jnp.sum(jnp.where(row == col, lower_right, 0), axis=0, keepdims=True)
    tile_row = lax.broadcasted_iota(jnp.int32, (8, HALF), 0)
    dst[3 * GROUP:TOP, :] = jnp.where(tile_row == 0, diagonal, exponent.astype(jnp.int32))
    for k, words in enumerate(to_words(whole[HALF:, :HALF])):
        dst[TOP + k * GROUP:TOP + (k + 1) * GROUP, :] = words


def decode_into(dst, coded):
    row, col = iotas(HALF)
    scale = jnp.exp2(coded[3 * GROUP + 1:3 * GROUP + 2, :].astype(F32)) * (1.0 / 8388608.0)
    both = from_words(coded[:3 * GROUP]).astype(F32) * scale
    diagonal = coded[3 * GROUP:3 * GROUP + 1, :].astype(F32) * scale
    below = from_words(coded[TOP:]).astype(F32) * scale
    turned = both.T
    dst[0:HALF, 0:HALF] = jnp.where(row >= col, both, turned)
    dst[HALF:BLOCK, HALF:BLOCK] = jnp.where(row < col, both, jnp.where(row == col, diagonal, turned))
    dst[HALF:BLOCK, 0:HALF] = below
    dst[0:HALF, HALF:BLOCK] = below.T


def bdot(a, b):
    return jnp.dot(a, b, preferred_element_type=F32)


def gram(v):
    return lax.dot_general(v, v, (((0,), (0,)), ((), ())), preferred_element_type=F32)


def split2(v):
    high = v.astype(BF16)
    return high, (v - high.astype(F32)).astype(BF16)


def split3(v):
    high = v.astype(BF16)
    rest = v - high.astype(F32)
    mid = rest.astype(BF16)
    return high, mid, (rest - mid.astype(F32)).astype(BF16)


def dot3(a, b):
    ah, al = split2(a)
    bh, bl = split2(b)
    return (bdot(ah, bl) + bdot(al, bh)) + bdot(ah, bh)


def newton_inverse(full, state, total_tokens):
    row, col = iotas(BLOCK)
    on_diagonal = row == col
    cov = full[...] * (1.0 / total_tokens)
    trace = jnp.sum(jnp.where(on_diagonal, cov, 0.0))
    damped = cov + jnp.where(on_diagonal, DAMPING / BLOCK * trace, 0.0)
    bound = jnp.max(jnp.sum(jnp.abs(damped), axis=0, keepdims=True), axis=1, keepdims=True)
    p = damped / bound
    state[BLOCK:, :] = jnp.where(on_diagonal, 2.0, 0.0) - p
    state[:BLOCK, :] = 2.0 * p - jnp.dot(p, p, precision=lax.Precision.HIGHEST)

    def sweep(fine, index, carry):
        p, x = state[:BLOCK, :], state[BLOCK:, :]
        ph, pm, pl_ = split3(p)
        xh, xm = split2(x)
        cross = bdot(pm, ph) + bdot(ph, pm)
        if fine:
            cross = (bdot(ph, pl_) + bdot(pl_, ph) + bdot(pm, pm)) + cross
        state[:BLOCK, :] = 2.0 * p - (cross + bdot(ph, ph))
        state[BLOCK:, :] = 2.0 * x - ((bdot(xm, ph) + bdot(xh, pm)) + bdot(xh, ph))
        return carry

    lax.fori_loop(0, NS_ITERS - 2 - COARSE, functools.partial(sweep, True), 0)
    lax.fori_loop(0, COARSE, functools.partial(sweep, False), 0)
    p, x = state[:BLOCK, :], state[BLOCK:, :]
    return (2.0 * x - dot3(x, p)) / bound


def factor_kernel(
    total_tokens,
    tokens,
    out_grads,
    gradient,
    a_all,
    g_all,
    right_high,
    right_low,
    tok,
    grads,
    grad_in,
    a_part,
    a_core,
    a_ring,
    a_sum,
    a_second,
    a_line,
    a_third,
    a_cross,
    g_part,
    g_core,
    g_ring,
    g_sum,
    g_other,
    ns_in,
    full,
    state,
    load_sem,
    send_sem,
    recv_sem,
):
    dp, tensor = lax.axis_index("dp"), lax.axis_index("tensor")
    x, y_lo, c = dp // 4, (dp // 2) % 2, dp % 2
    y_hi, z = tensor // 4, tensor % 4
    y = y_hi * 2 + y_lo
    o = 1 - c

    def device(x_, y_, z_, c_):
        return {"dp": x_ * 4 + (y_ % 2) * 2 + c_, "tensor": (y_ // 2) * 4 + z_}

    def turn(position, by):
        return (position + by) % 4

    first, second = o * z + c * y, o * y + c * z

    def plane(first_, second_):
        return device(x, c * first_ + o * second_, o * first_ + c * second_, c)

    other_core = device(x, y, z, o)
    y_partner = y_hi * 2 + 1 - y_lo

    def a_core_of(y_, z_):
        return (y_ + z_ + 1) % 2

    on_a = c == a_core_of(y, z)
    on_g = jnp.logical_not(on_a)

    sent = []
    counters = {"send": 0, "recv": 0}

    def take(kind, count=1):
        at = counters[kind]
        counters[kind] += count
        return at

    def send(src, dst, recv_at, target, cond=None):
        send_at = take("send")

        def make():
            return pltpu.make_async_remote_copy(
                src_ref=src, dst_ref=dst, send_sem=send_sem.at[send_at], recv_sem=recv_sem.at[recv_at],
                device_id=target, device_id_type=MESH,
            )

        if cond is None:
            make().start()
        else:
            pl.when(cond)(lambda: make().start())
        sent.append((send_at, src.shape, cond))

    def await_recv(dst, recv_at):
        pltpu.make_async_remote_copy(
            src_ref=dst, dst_ref=dst, send_sem=send_sem.at[0], recv_sem=recv_sem.at[recv_at],
            device_id=other_core, device_id_type=MESH,
        ).wait_recv()

    def wait_sent(send_at, shape):
        like = {
            (ROWS, HALF): g_sum,
            (PIECE, HALF): a_line,
            (4, PIECE, HALF): a_sum,
            (CODED, HALF): a_all.at[0],
            (TOP, HALF): a_all.at[0, 0:TOP],
            (CODED - TOP, HALF): a_all.at[0, TOP:CODED],
        }[tuple(shape)]
        pltpu.make_async_remote_copy(
            src_ref=like, dst_ref=like, send_sem=send_sem.at[send_at], recv_sem=recv_sem.at[0],
            device_id=other_core, device_id_type=MESH,
        ).wait_send()

    def finish():
        for send_at, shape, cond in sent:
            if cond is None:
                wait_sent(send_at, shape)
            else:
                pl.when(cond)(functools.partial(wait_sent, send_at, shape))

    barrier = pltpu.get_barrier_semaphore()
    others = []
    for by in (2, 1, 3):
        others.append(device(turn(x, by), y, z, c))
        others.append(device(turn(x, by), y, z, o))
        others.append(device(x, turn(y, by), z, c))
        others.append(device(x, y, turn(z, by), c))
    for by in (1, 3):
        others.append(device(x, turn(y, by), z, o))
        others.append(device(x, y, turn(z, by), o))
    others.append(other_core)
    for target in others:
        pl.semaphore_signal(barrier, inc=1, device_id=target, device_id_type=MESH)

    token_load = pltpu.make_async_copy(tokens, tok, load_sem.at[8])
    token_load.start()
    gradient_load = pltpu.make_async_copy(gradient, grad_in, load_sem.at[9])

    def grad_load(at):
        by = (2, 1, 3, 0)[at % 4]
        core = o + (at // 4) * (c - o)
        block = 2 * turn(x, by) + (core + z) % 2
        return pltpu.make_async_copy(
            out_grads.at[:, pl.ds(pl.multiple_of(block * BLOCK, BLOCK), BLOCK)], grads.at[at], load_sem.at[at]
        )


    def grad_waits(stage):
        gradient_load.wait()
        for at in range(8):
            if stage == 1 or (stage <= 3 and at >= 4):
                grad_load(at).wait()

    token_load.wait()
    for at in range(8):
        grad_load(at).start()
    gradient_load.start()

    def a_gram(k, carry):
        v = tok[:, pl.ds(pl.multiple_of(k * BLOCK, BLOCK), BLOCK)]
        pack_into(a_part.at[0, k % 4, k // 4], a_part.at[1, k // 4, k % 4], gram(v))
        return carry

    lax.fori_loop(0, 16, a_gram, 0, unroll=4)
    pl.semaphore_wait(barrier, len(others))

    a_core_recv = take("recv", 4)
    orders = (2, 1, 3, 0)
    for i in range(4):
        at = turn(first, orders[i])
        send(a_part.at[o, :, at], a_core.at[:, at], a_core_recv + i, other_core)

    g_core_recv = take("recv", 4)

    def g_gram(at):
        grad_load(at).wait()
        pack_into(g_part.at[at, 0:PIECE], g_part.at[at, PIECE:ROWS], gram(grads[at]))

    def their_gram(i):
        g_gram(i)
        send(g_part.at[i], g_core.at[i], g_core_recv + i, other_core)

    their_gram(0)
    their_gram(1)

    a_ring_recv = take("recv", 12)
    for i in range(4):
        at = turn(second, orders[i])
        await_recv(a_core.at[:, at], a_core_recv + i)
        a_part[c, :, at] += a_core[:, at]
        for by in (2, 1, 3):
            send(
                a_part.at[c, turn(first, by), at], a_ring.at[3 - by, at], a_ring_recv + 3 * i + 3 - by,
                plane(turn(first, by), second),
            )

    their_gram(2)
    their_gram(3)

    g_ring_recv = take("recv", 3)
    for i in range(4):
        g_gram(4 + i)
        await_recv(g_core.at[i], g_core_recv + i)
        g_part[4 + i] += g_core[i]
        if i < 3:
            slot = 3 - orders[i]
            send(g_part.at[4 + i], g_ring.at[slot], g_ring_recv + slot, device(turn(x, orders[i]), y, z, c))

    a_second_recv = take("recv", 3)
    for i in range(4):
        at = turn(second, orders[i])
        for slot in range(3):
            await_recv(a_ring.at[slot, at], a_ring_recv + 3 * i + slot)
        a_sum[i] = (a_part[c, first, at] + a_ring[0, at]) + (a_ring[1, at] + a_ring[2, at])
        if i < 3:
            slot = 3 - orders[i]
            send(a_sum.at[i], a_second.at[slot], a_second_recv + slot, plane(first, at))

    for slot in range(3):
        await_recv(g_ring.at[slot], g_ring_recv + slot)
    g_sum[...] = (g_part[7] + g_ring[0]) + (g_ring[1] + g_ring[2])
    g_y_recv = take("recv")
    send(g_sum, g_other, g_y_recv, device(x, y_partner, z, c), on_a)

    for slot in range(3):
        await_recv(a_second.at[slot], a_second_recv + slot)
    a_line[...] = (a_sum[3] + a_second[0]) + (a_second[1] + a_second[2])
    a_third_recv = take("recv", 6)
    a_cross_recv = take("recv")
    for by in (2, 1, 3):
        send(
            a_line, a_third.at[3 - by, c], a_third_recv + 2 * (3 - by) + c,
            device(turn(x, by), y, z, a_core_of(y, z)),
        )
    send(a_line, a_cross, a_cross_recv, other_core, on_g)

    @pl.when(on_g)
    def _():
        await_recv(g_other, g_y_recv)
        ns_in[...] = g_sum[...] + g_other[...]

    @pl.when(on_a)
    def _():
        await_recv(a_cross, a_cross_recv)
        for slot in range(3):
            for h in range(2):
                await_recv(a_third.at[slot, h], a_third_recv + 2 * slot + h)
        here = pl.ds(pl.multiple_of(c * PIECE, 8), PIECE)
        there = pl.ds(pl.multiple_of(o * PIECE, 8), PIECE)
        ns_in[here] = (a_line[...] + a_third[0, c]) + (a_third[1, c] + a_third[2, c])
        ns_in[there] = (a_cross[...] + a_third[0, o]) + (a_third[1, o] + a_third[2, o])

    g_mine = 2 * x + y_lo
    a_mine = 4 * y + z
    unpack_into(full, ns_in[...])
    full[...] = newton_inverse(full, state, total_tokens)

    g_x_recv = take("recv", 9)
    g_p_recv = take("recv", 2)
    g_copy_recv = take("recv", 8)
    g_sends = len(sent)

    @pl.when(on_g)
    def _():
        encode_into(g_all.at[g_mine], full[...])
        own = g_all.at[g_mine]
        halves = (pl.ds(0, TOP), pl.ds(TOP, CODED - TOP))
        for h, rows in enumerate(halves):
            send(own.at[rows], own.at[rows], g_p_recv + h, device(x, y_partner, z, o))
        for by in (1, 3, 2):
            send(own, own, g_x_recv + 3 - by, device(turn(x, by), y, z, c))
        send(own, own, g_copy_recv + g_mine, other_core)
        beside = 2 * x + 1 - y_lo
        held = g_all.at[beside]
        for h, rows in enumerate(halves):
            await_recv(held.at[rows], g_p_recv + h)
            for by in (1, 3, 2):
                send(held.at[rows], held.at[rows], g_x_recv + 3 + 3 * h + 3 - by, device(turn(x, by), y, z, c))
        send(held, held, g_copy_recv + beside, other_core)
        for slot in (0, 2, 1):
            block = 2 * turn(x, 1 + slot) + y_lo
            held = g_all.at[block]
            await_recv(held, g_x_recv + slot)
            send(held, held, g_copy_recv + block, other_core)
        for slot in (0, 2, 1):
            block = 2 * turn(x, 1 + slot) + 1 - y_lo
            held = g_all.at[block]
            for h, rows in enumerate(halves):
                await_recv(held.at[rows], g_x_recv + 3 + 3 * h + slot)
            send(held, held, g_copy_recv + block, other_core)

    g_sends = (g_sends, len(sent))

    a_y_recv = take("recv", 6)
    a_z_recv = take("recv", 6)
    a_top_recv = take("recv", 9)
    a_bottom_recv = take("recv", 9)
    a_copy_recv = take("recv", 16)
    a_sends = len(sent)

    def to_y(by):
        y_ = turn(y, by)
        return device(x, y_, z, a_core_of(y_, z))

    def to_z(by):
        z_ = turn(z, by)
        return device(x, y, z_, a_core_of(y, z_))

    @pl.when(on_a)
    def _():
        encode_into(a_all.at[a_mine], full[...])
        own = a_all.at[a_mine]
        own_top, own_bottom = a_all.at[a_mine, 0:TOP], a_all.at[a_mine, TOP:CODED]
        for by in (1, 3, 2):
            send(own_top, own_top, a_y_recv + 3 - by, to_y(by))
            send(own_bottom, own_bottom, a_z_recv + 3 - by, to_z(by))
        for by in (1, 3, 2):
            send(own_bottom, own_bottom, a_y_recv + 6 - by, to_y(by))
            send(own_top, own_top, a_z_recv + 6 - by, to_z(by))
        send(own, own, a_copy_recv + a_mine, other_core)
        for slot in (0, 2, 1):
            top = a_all.at[4 * turn(y, 1 + slot) + z, 0:TOP]
            await_recv(top, a_y_recv + slot)
            for by in (1, 3, 2):
                send(top, top, a_top_recv + 3 * slot + 3 - by, to_z(by))
            bottom = a_all.at[4 * y + turn(z, 1 + slot), TOP:CODED]
            await_recv(bottom, a_z_recv + slot)
            for by in (1, 3, 2):
                send(bottom, bottom, a_bottom_recv + 3 * slot + 3 - by, to_y(by))
        for slot in (0, 2, 1):
            block = 4 * turn(y, 1 + slot) + z
            await_recv(a_all.at[block, TOP:CODED], a_y_recv + 3 + slot)
            send(a_all.at[block], a_all.at[block], a_copy_recv + block, other_core)
            block = 4 * y + turn(z, 1 + slot)
            await_recv(a_all.at[block, 0:TOP], a_z_recv + 3 + slot)
            send(a_all.at[block], a_all.at[block], a_copy_recv + block, other_core)

    gradient_load.wait()

    def right_product(i, carry):
        j = 2 * turn(x, i % 4) + y_lo + (i // 4) * (1 - 2 * y_lo)

        @pl.when(on_a)
        def _():
            await_recv(g_all.at[j], g_copy_recv + j)

        columns = pl.ds(pl.multiple_of(j * BLOCK, BLOCK), BLOCK)
        decode_into(full, g_all[j])
        right_high[:, columns], right_low[:, columns] = split2(dot3(grad_in[:, columns], full[...]))
        return carry

    lax.fori_loop(0, 8, right_product, 0)

    @pl.when(on_a)
    def _():
        for slot_y in (0, 2, 1):
            for slot_z in (0, 2, 1):
                block = 4 * turn(y, 1 + slot_y) + turn(z, 1 + slot_z)
                await_recv(a_all.at[block, 0:TOP], a_top_recv + 3 * slot_y + slot_z)
                await_recv(a_all.at[block, TOP:CODED], a_bottom_recv + 3 * slot_z + slot_y)
                send(a_all.at[block], a_all.at[block], a_copy_recv + block, other_core)

    a_sends = (a_sends, len(sent))

    @pl.when(on_g)
    def _():
        def copied(block, carry):
            await_recv(a_all.at[block], a_copy_recv + block)
            return carry

        lax.fori_loop(0, 16, copied, 0)

    for (start, stop), held_here in ((g_sends, on_g), (a_sends, on_a)):
        for index in range(start, stop):
            sent[index] = (*sent[index][:2], held_here)
    finish()


def factors(tokens, out_grads, gradient, total_tokens):
    vmem = pl.BlockSpec(memory_space=pltpu.VMEM)
    anywhere = pl.BlockSpec(memory_space=pltpu.HBM)

    def pieces(*lead):
        return pltpu.VMEM((*lead, PIECE, HALF), F32)

    def blocks(*lead):
        return pltpu.VMEM((*lead, ROWS, HALF), F32)

    tokens, out_grads, gradient = (
        pltpu.with_memory_space_constraint(v, pltpu.HBM) for v in (tokens, out_grads, gradient)
    )
    return pl.pallas_call(
        functools.partial(factor_kernel, total_tokens),
        out_shape=(
            jax.ShapeDtypeStruct((16, CODED, HALF), jnp.int32),
            jax.ShapeDtypeStruct((8, CODED, HALF), jnp.int32),
            jax.ShapeDtypeStruct(gradient.shape, BF16),
            jax.ShapeDtypeStruct(gradient.shape, BF16),
        ),
        in_specs=[anywhere, anywhere, anywhere],
        out_specs=(vmem, vmem, vmem, vmem),
        scratch_shapes=[
            pltpu.VMEM(tokens.shape, BF16),
            pltpu.VMEM((8, 2048, BLOCK), BF16),
            pltpu.VMEM(gradient.shape, F32),
            pieces(2, 4, 4),
            pieces(4, 4),
            pieces(3, 4),
            pieces(4),
            pieces(3),
            pieces(),
            pieces(3, 2),
            pieces(),
            blocks(8),
            blocks(4),
            blocks(3),
            blocks(),
            blocks(),
            blocks(),
            pltpu.VMEM((BLOCK, BLOCK), F32),
            pltpu.VMEM((2 * BLOCK, BLOCK), F32),
            pltpu.SemaphoreType.DMA((10,)),
            pltpu.SemaphoreType.DMA((128,)),
            pltpu.SemaphoreType.DMA((128,)),
        ],
        compiler_params=pltpu.CompilerParams(
            collective_id=0, has_side_effects=True, vmem_limit_bytes=32 * 2**20
        ),
        name="factors",
    )(tokens, out_grads, gradient)


def apply_kernel(owners, a_all, g_all, right_high, right_low, out, inverses, left, result, placed, out_sem):
    dp = lax.axis_index("dp")
    width = right_high.shape[1] // 4
    decode_into(left, a_all[dp])

    def out_copy(q):
        columns = pl.ds(pl.multiple_of(q * width, width), width)
        return pltpu.make_async_copy(result.at[:, columns], out.at[:, columns], out_sem.at[q])

    left_high, left_low = split2(left[...])

    def left_product(q, carry):
        columns = pl.ds(pl.multiple_of(q * width, width), width)
        high = right_high[:, columns]
        result[:, columns] = (bdot(left_high, right_low[:, columns]) + bdot(left_low, high)) + bdot(left_high, high)
        out_copy(q).start()
        return carry

    lax.fori_loop(0, 4, left_product, 0, unroll=4)

    def scan(b, carry):
        seen, slots = carry
        hit = owners[0, b] == dp
        slots = tuple(jnp.where(jnp.logical_and(hit, seen == s), b, slot) for s, slot in enumerate(slots))
        return seen + hit.astype(jnp.int32), slots

    _, slots = lax.fori_loop(0, 24, scan, (jnp.int32(0), (jnp.int32(-1),) * 3), unroll=8)
    for s, chosen in enumerate(slots):
        @pl.when(chosen < 0)
        def _():
            placed[s] = jnp.zeros((BLOCK, BLOCK), F32)

        @pl.when(jnp.logical_and(chosen >= 0, chosen < 16))
        def _():
            decode_into(placed.at[s], a_all[chosen])

        @pl.when(chosen >= 16)
        def _():
            decode_into(placed.at[s], g_all[chosen - 16])

        pltpu.make_async_copy(placed.at[s], inverses.at[0, 0, s], out_sem.at[4 + s]).start()
    for q in range(4):
        out_copy(q).wait()
    for s in range(3):
        pltpu.make_async_copy(placed.at[s], inverses.at[0, 0, s], out_sem.at[4 + s]).wait()


def apply(owners, a_all, g_all, right_high, right_low):
    vmem = pl.BlockSpec(memory_space=pltpu.VMEM)
    anywhere = pl.BlockSpec(memory_space=pl.ANY)
    return pl.pallas_call(
        apply_kernel,
        out_shape=(
            jax.ShapeDtypeStruct(right_high.shape, F32),
            jax.ShapeDtypeStruct((1, 1, 3, BLOCK, BLOCK), F32),
        ),
        in_specs=[pl.BlockSpec(memory_space=pltpu.SMEM), vmem, vmem, vmem, vmem],
        out_specs=(anywhere, anywhere),
        scratch_shapes=[
            pltpu.VMEM((BLOCK, BLOCK), F32),
            pltpu.VMEM(right_high.shape, F32),
            pltpu.VMEM((3, BLOCK, BLOCK), F32),
            pltpu.SemaphoreType.DMA((7,)),
        ],
        compiler_params=pltpu.CompilerParams(vmem_limit_bytes=32 * 2**20),
        name="apply",
    )(owners, a_all, g_all, right_high, right_low)


def on_device(tokens, out_grads, gradient, owners):
    total_tokens = tokens.shape[0] * lax.axis_size("tensor") * lax.axis_size("dp")
    return apply(owners, *factors(tokens, out_grads, gradient, total_tokens))


def solution(mesh):
    placed = (P(("dp", "tensor"), None), P("dp", "tensor"), P("dp", "tensor"), P("tensor", None))
    return jax.shard_map(
        on_device,
        mesh=mesh,
        in_specs=placed,
        out_specs=(P("dp", "tensor"), P("tensor", "dp", None, None, None)),
        check_vma=False,
    )
```
